512 devices in a mesh: seq: 128 (over z, y, core), head: 4 (over x).
Axes of the slice: x: 4, y: 4, z: 16, core: 2. Of those that a mesh axis runs over, the one named last changes fastest.
Arguments:
- queries: bfloat16 [73728, 512], P('seq', 'head'), may hold values from -16 to 16, as said below
- key_states: bfloat16 [73728, 512], P('seq', 'head'), may hold values from -5 to 5, as said below
- value_states: bfloat16 [73728, 512], P('seq', 'head'), may hold values from -8 to 8
- out_weight: bfloat16 [512, 1024], P(None, 'head'), may hold values from -0.25 to 0.25
- output_grad: bfloat16 [73728, 1024], P('seq', 'head'), may hold values from -6 to 6
- rand_blocks: int32 [1152, 3], P('seq'), may hold values from 0 to 1151, as said below
- global_pos: int32 [128], replicated, may hold values from 0 to 73727, as said below
Outputs:
- projected: bfloat16 [73728, 1024], P('seq', 'head')
- query_grad: bfloat16 [73728, 512], P('seq', 'head')
- key_grad: bfloat16 [73728, 512], P('seq', 'head')
- value_grad: bfloat16 [73728, 512], P('seq', 'head')
- weight_grad: float32 [512, 1024], P(None, 'head')
The draws below stay inside these ranges and needn't reach their ends.
Inputs may be any that keep to these rules, and one draw needn't show every extreme that they name: `queries`: queries drawn for attention, of either sign. `key_states`: keys drawn for attention, of either sign. `rand_blocks`: block indices. Among the 27 entries of the 9 query blocks of one index of seq, no two name blocks of the same index of seq (block // 9); in every draw some index of seq has exactly 1 of its blocks named by the entries of every index of seq. `global_pos`: distinct token positions.
All inputs are finite; a program needn't handle non-finite values.
Results may differ from the reference program's by a relative error of at most 0.038.
Values may be sent and summed in bfloat16 or wider, within the bound.
No kernel may reach another device: no remote copies, remote signals or barrier semaphores. Data moves between devices by JAX's collectives and lax.ppermute only.
A program may use at most 128 MiB of HBM per device.

```python
import math
import jax
import jax.numpy as jnp
from jax import lax

HEADS = 8
HEAD_DIM = 64
D = 1024
BLOCK = 64
R = 3
G = 128
QBLK = 9
REQ = 27
TOKENS = 73728
NBLK = 1152
CAP = 1
COLS = 512
N_SEQ = 128


def shared_parts(key):
    base_queries = jax.random.normal(jax.random.fold_in(key, 101), (TOKENS, COLS), jnp.float32)
    base_keys = jax.random.normal(jax.random.fold_in(key, 102), (TOKENS, COLS), jnp.float32)
    return (base_queries, base_keys)


def draw_queries(key, part):
    base_queries, base_keys = shared_parts(key)
    drawn = jnp.clip(base_queries * 1.1, -4.4, 4.4)
    return drawn.astype(jnp.bfloat16)


def draw_key_states(key, part):
    base_queries, base_keys = shared_parts(key)
    drawn = jnp.clip(base_keys * 1.1, -4.4, 4.4)
    return drawn.astype(jnp.bfloat16)


def draw_rand_blocks(key, part):
    key = jax.random.fold_in(key, 3)
    hot_owner = jax.random.randint(jax.random.fold_in(key, 0), (), 0, N_SEQ)

    def one_device(device):
        device_key = jax.random.fold_in(key, device + 1)
        first_key, second_key, third_key = jax.random.split(device_key, 3)
        spread = jax.random.permutation(first_key, (N_SEQ - 1) * CAP)[:REQ - CAP] // CAP
        spread = spread + (spread >= hot_owner).astype(spread.dtype)
        owners = jnp.concatenate([jnp.full((CAP,), hot_owner, jnp.int32), spread.astype(jnp.int32)])
        owners = owners[jax.random.permutation(second_key, REQ)]
        inside_block = jax.random.randint(third_key, (REQ,), 0, QBLK)
        return (owners * QBLK + inside_block).reshape(QBLK, R)
    return jax.vmap(one_device)(jnp.arange(N_SEQ)).reshape(NBLK, R).astype(jnp.int32)


def draw_global_pos(key, part):
    key = jax.random.fold_in(key, 4)
    return jax.random.permutation(key, TOKENS)[:G].astype(jnp.int32)


def block_scale(key, shape, pieces, smallest, top_value):
    def one(dim, parts):
        heights = jax.random.uniform(jax.random.fold_in(jax.random.fold_in(key, 6), dim), (parts,), jnp.float32, smallest / len(pieces), top_value / len(pieces))
        return jnp.repeat(jnp.exp(heights), shape[dim] // parts).reshape((-1,) + (1,) * (len(shape) - dim - 1))

    gain = one(*pieces[0])
    for cut in pieces[1:]:
        gain = gain * one(*cut)
    return gain


def gaussian(stream_key, dims, scale, bound, pieces=(), kind=jnp.bfloat16):
    drawn = scale * jax.random.normal(stream_key, dims, jnp.float32)
    if pieces:
        drawn = drawn * block_scale(stream_key, dims, pieces, -0.22, 0.18)
    return jnp.clip(drawn, -bound, bound).astype(kind)


def setup_inputs(seed: int = 0) -> dict:
    arg_keys = jax.random.split(jax.random.key(seed), 8)
    queries = draw_queries(jax.random.fold_in(arg_keys[7], 71), 0)
    key_states = draw_key_states(jax.random.fold_in(arg_keys[7], 71), 0)
    value_states = gaussian(arg_keys[2], (TOKENS, COLS), 2.0, 8.0, ((0, 128), (1, 4)))
    out_weight = gaussian(arg_keys[3], (COLS, D), COLS ** -0.5, 0.25, ((1, 4),))
    output_grad = gaussian(arg_keys[4], (TOKENS, D), 1.0, 6.0, ((0, 128), (1, 4)))
    rand_blocks = draw_rand_blocks(jax.random.fold_in(arg_keys[7], 71), 0)
    global_pos = draw_global_pos(jax.random.fold_in(arg_keys[7], 71), 0)
    return {"queries": queries, "key_states": key_states, "value_states": value_states, "out_weight": out_weight, "output_grad": output_grad, "rand_blocks": rand_blocks, "global_pos": global_pos}


def head_split(matrix):
    return matrix.reshape(matrix.shape[0], matrix.shape[1], HEADS, HEAD_DIM)

def reference(queries, key_states, value_states, out_weight, output_grad, rand_blocks, global_pos):
    score_scale = 1.0 / math.sqrt(HEAD_DIM)
    grad_att = jnp.dot(output_grad, out_weight.T, preferred_element_type=jnp.float32).astype(jnp.bfloat16)
    group_blocks = math.gcd(NBLK, 64)
    groups = NBLK // group_blocks
    inside = jnp.arange(BLOCK, dtype=jnp.int32)

    def group_step(carry_sums, group_index):
        key_acc, value_acc = carry_sums
        blocks = group_index * group_blocks + jnp.arange(group_blocks, dtype=jnp.int32)
        window_rows = []
        window_live = []
        for shift_by in (-1, 0, 1):
            neighbour = blocks + shift_by
            neighbour_live = (neighbour >= 0) & (neighbour < NBLK)
            window_rows.append(jnp.clip(neighbour, 0, NBLK - 1)[:, None] * BLOCK + inside[None, :])
            window_live.append(jnp.broadcast_to(neighbour_live[:, None], (group_blocks, BLOCK)))
        random_picks = lax.dynamic_slice_in_dim(rand_blocks, group_index * group_blocks, group_blocks, 0)
        random_rows = (random_picks[:, :, None] * BLOCK + inside[None, None, :]).reshape(group_blocks, R * BLOCK)
        global_rows = jnp.broadcast_to(global_pos[None, :], (group_blocks, G))
        key_index = jnp.concatenate(window_rows + [global_rows, random_rows], axis=1).astype(jnp.int32)
        key_live = jnp.concatenate(window_live + [jnp.ones((group_blocks, G + R * BLOCK), bool)], axis=1)
        query_rows = (blocks[:, None] * BLOCK + inside[None, :]).astype(jnp.int32)
        block_query = head_split(queries[query_rows].astype(jnp.float32))
        block_grad = head_split(grad_att[query_rows].astype(jnp.float32))
        block_key = head_split(key_states[key_index].astype(jnp.float32))
        block_value = head_split(value_states[key_index].astype(jnp.float32))
        scores = jnp.einsum('bqhd,bkhd->bhqk', block_query, block_key) * score_scale
        scores = jnp.where(key_live[:, None, None, :], scores, -jnp.inf)
        row_top = lax.optimization_barrier(jnp.max(scores, axis=-1, keepdims=True))
        log_total = row_top + jnp.log(lax.optimization_barrier(jnp.sum(jnp.exp(scores - row_top), axis=-1, keepdims=True)))
        probs = jnp.exp(scores - log_total)
        probs_b = lax.optimization_barrier(probs.astype(jnp.bfloat16)).astype(jnp.float32)
        attended = jnp.einsum('bhqk,bkhd->bqhd', probs_b, block_value).astype(jnp.bfloat16)
        delta = jnp.einsum('bqhd,bqhd->bhq', block_grad, attended.astype(jnp.float32))[..., None]
        dprob = jnp.einsum('bqhd,bkhd->bhqk', block_grad, block_value)
        dscore = probs * (dprob - delta)
        dscore_b = lax.optimization_barrier(dscore.astype(jnp.bfloat16)).astype(jnp.float32)
        query_grad = (score_scale * jnp.einsum('bhqk,bkhd->bqhd', dscore_b, block_key)).astype(jnp.bfloat16)
        key_part = score_scale * jnp.einsum('bhqk,bqhd->bkhd', dscore_b, block_query)
        value_part = jnp.einsum('bhqk,bqhd->bkhd', probs_b, block_grad)
        flat_index = key_index.reshape(-1)
        key_acc = key_acc.at[flat_index].add(key_part.reshape(-1, COLS))
        value_acc = value_acc.at[flat_index].add(value_part.reshape(-1, COLS))
        return ((key_acc, value_acc), (attended.reshape(group_blocks * BLOCK, COLS), query_grad.reshape(group_blocks * BLOCK, COLS)))
    zero_rows = jnp.zeros((TOKENS, COLS), jnp.float32)
    sums, outputs = lax.scan(group_step, (zero_rows, zero_rows), jnp.arange(groups, dtype=jnp.int32))
    attended = outputs[0].reshape(TOKENS, COLS)
    query_grad = outputs[1].reshape(TOKENS, COLS)
    projected = jnp.dot(attended, out_weight, preferred_element_type=jnp.float32).astype(jnp.bfloat16)
    weight_grad = jnp.dot(attended.T, output_grad, preferred_element_type=jnp.float32) * (1.0 / math.sqrt(TOKENS))
    return (projected, query_grad, sums[0].astype(jnp.bfloat16), sums[1].astype(jnp.bfloat16), weight_grad)
```

```python
import math

import jax
import jax.numpy as jnp
from jax import lax
from jax.experimental import pallas as pl
from jax.experimental.pallas import tpu as pltpu
from jax.sharding import Mesh
from jax.sharding import PartitionSpec as P

HEAD_DIM = 64
BLOCK = 64
PAIR = 2 * BLOCK
R = 3
GLOBALS = 128
LANES = 8
TILE = 16
VMEM_LIMIT = 40 * 1024 * 1024


def whole(space=pltpu.VMEM):
    return pl.BlockSpec(memory_space=space)


def shape(dims, dtype):
    return jax.ShapeDtypeStruct(dims, dtype)


def call(kernel, out_shape, in_specs, scratch=(), flops=0, moved=0):
    return pl.pallas_call(
        kernel,
        out_shape=out_shape,
        in_specs=in_specs,
        out_specs=jax.tree.map(lambda _: whole(), out_shape),
        scratch_shapes=list(scratch),
        compiler_params=pltpu.CompilerParams(vmem_limit_bytes=VMEM_LIMIT),
        cost_estimate=pl.CostEstimate(flops=flops, bytes_accessed=moved, transcendentals=0),
    )


def serve_kernel(where, asked, global_pos, lane_blocks, send, panel):
    me, slab = where[0], where[1]
    slabs, blocks = lane_blocks.shape[:2]
    tokens = blocks * BLOCK

    def serve(number, carry):
        to = number // slabs
        source = number % slabs
        send[to, source] = lane_blocks[source, jnp.maximum(asked[number], 0)]
        return carry

    lax.fori_loop(0, LANES * slabs, serve, 0)

    panel[...] = jnp.zeros_like(panel)
    row_number = lax.broadcasted_iota(jnp.int32, (TILE, panel.shape[1]), 0)

    def pick(number, carry):
        position = global_pos[number]
        owner = position // tokens
        row = position % tokens

        @pl.when(owner % LANES == me)
        def _():
            source, block, inside = owner // LANES, row // BLOCK, row % BLOCK
            first = pl.multiple_of(inside // TILE * TILE, TILE)
            hit = row_number == inside % TILE
            for half in range(2):
                rows = lane_blocks[source, block, pl.ds(first + half * BLOCK, TILE), :]
                line = jnp.sum(
                    jnp.where(hit, rows.astype(jnp.float32), 0.0), axis=0, keepdims=True
                )
                panel[pl.ds(number + half * GLOBALS, 1), :] = line

        return carry

    lax.fori_loop(0, GLOBALS, pick, 0)
    panel_rows = panel[...].astype(send.dtype).reshape(2, PAIR, panel.shape[1])

    def rest(to, carry):
        send[to, slabs : slabs + 2] = panel_rows
        to_right = to == (me + 1) % LANES
        source = jnp.where(
            to_right,
            jnp.where(me == LANES - 1, slab - 1, slab),
            jnp.where(me == 0, slab + 1, slab),
        )
        source = jnp.clip(source, 0, slabs - 1)
        send[to, slabs + 2] = lane_blocks[source, jnp.where(to_right, blocks - 1, 0)]
        return carry

    lax.fori_loop(0, LANES, rest, 0)


def attention_kernel(
    where,
    names,
    q,
    g,
    key,
    value,
    arrived,
    attended,
    query_grad,
    key_grad,
    value_grad,
    send,
    key_pad,
    value_pad,
    panel,
    panel_grad,
):
    me, slab = where[0], where[1]
    slabs = arrived.shape[1] - 3
    tokens, columns = q.shape
    blocks = tokens // BLOCK
    scale = 1.0 / math.sqrt(HEAD_DIM)
    f32, bf16 = jnp.float32, jnp.bfloat16
    left_lane, right_lane = (me + LANES - 1) % LANES, (me + 1) % LANES
    key_pad[:BLOCK, :] = arrived[left_lane, slabs + 2, :BLOCK, :]
    value_pad[:BLOCK, :] = arrived[left_lane, slabs + 2, BLOCK:, :]
    key_pad[BLOCK : BLOCK + tokens, :] = key[...]
    value_pad[BLOCK : BLOCK + tokens, :] = value[...]
    key_pad[BLOCK + tokens :, :] = arrived[right_lane, slabs + 2, :BLOCK, :]
    value_pad[BLOCK + tokens :, :] = arrived[right_lane, slabs + 2, BLOCK:, :]
    panel_sum = jnp.zeros((2, PAIR, columns), f32)
    for lane in range(LANES):
        panel_sum += arrived[lane, slabs : slabs + 2].astype(f32)
    panel[...] = panel_sum.astype(bf16)
    key_grad[...] = jnp.zeros_like(key_grad)
    value_grad[...] = jnp.zeros_like(value_grad)
    panel_grad[...] = jnp.zeros_like(panel_grad)
    first_block = (slab * LANES + me) * blocks
    last_block = slabs * LANES * blocks - 1
    first_head = lax.broadcasted_iota(jnp.int32, (BLOCK, columns), 1) < HEAD_DIM
    window = 3 * BLOCK
    keys = window + GLOBALS + R * BLOCK
    key_column = lax.broadcasted_iota(jnp.int32, (1, keys), 1)

    def by_head(rows):
        zero = jnp.zeros_like(rows)
        return jnp.concatenate(
            [jnp.where(first_head, rows, zero), jnp.where(first_head, zero, rows)], axis=0
        )

    def joined(pair):
        return jnp.where(first_head, pair[:BLOCK], pair[BLOCK:])

    def dot(a, b, dims):
        return lax.dot_general(a, b, (dims, ((), ())), preferred_element_type=f32)

    def one(block, carry):
        row = pl.multiple_of(block * BLOCK, BLOCK)
        here = pl.ds(row, BLOCK)
        around = pl.ds(row, window)
        owners = [names[block * R + j] // blocks for j in range(R)]
        slots = [(owner % LANES, owner // LANES) for owner in owners]
        kk = jnp.concatenate(
            [key_pad[around, :], panel[0]] + [arrived[a, b, :BLOCK, :] for a, b in slots], axis=0
        )
        vv = jnp.concatenate(
            [value_pad[around, :], panel[1]] + [arrived[a, b, BLOCK:, :] for a, b in slots], axis=0
        )
        q2 = by_head(q[here, :])
        g2 = by_head(g[here, :])
        number = first_block + block
        dead = ((key_column < BLOCK) & (number == 0)) | (
            (key_column >= 2 * BLOCK) & (key_column < window) & (number == last_block)
        )
        scores = dot(q2, kk, ((1,), (1,))) * scale
        scores = jnp.where(dead, -jnp.inf, scores)
        top = jnp.max(scores, axis=-1, keepdims=True)
        raised = jnp.exp(scores - top)
        probs = raised * (1.0 / jnp.sum(raised, axis=-1, keepdims=True))
        probs_b = probs.astype(bf16)
        att = joined(dot(probs_b, vv, ((1,), (0,)))).astype(bf16)
        attended[here, :] = att
        att_f = att.astype(f32)
        delta = jnp.sum(
            g2.astype(f32) * jnp.concatenate([att_f, att_f], axis=0), axis=-1, keepdims=True
        )
        slope = (probs * (dot(g2, vv, ((1,), (1,))) - delta)).astype(bf16)
        query_grad[here, :] = (scale * joined(dot(slope, kk, ((1,), (0,))))).astype(bf16)
        dk = scale * dot(slope, q2, ((0,), (0,)))
        dv = dot(probs_b, g2, ((0,), (0,)))
        key_grad[around, :] += dk[:window]
        value_grad[around, :] += dv[:window]
        panel_grad[0] += dk[window : window + GLOBALS]
        panel_grad[1] += dv[window : window + GLOBALS]
        for j, (a, b) in enumerate(slots):
            first = window + GLOBALS + j * BLOCK
            send[a, b, :BLOCK, :] = dk[first : first + BLOCK].astype(bf16)
            send[a, b, BLOCK:, :] = dv[first : first + BLOCK].astype(bf16)
        return carry

    lax.fori_loop(0, blocks, one, 0)
    panel_rows = panel_grad[...].astype(bf16)
    for lane in range(LANES):
        send[lane, slabs : slabs + 2] = panel_rows
    send[left_lane, slabs + 2, :BLOCK, :] = key_grad[:BLOCK, :].astype(bf16)
    send[left_lane, slabs + 2, BLOCK:, :] = value_grad[:BLOCK, :].astype(bf16)
    send[right_lane, slabs + 2, :BLOCK, :] = key_grad[BLOCK + tokens :, :].astype(bf16)
    send[right_lane, slabs + 2, BLOCK:, :] = value_grad[BLOCK + tokens :, :].astype(bf16)


def collect_kernel(where, asked, global_pos, returned, lane_grads, sums, panel):
    me, slab = where[0], where[1]
    slabs, blocks = lane_grads.shape[:2]
    tokens = blocks * BLOCK
    f32 = jnp.float32
    sums[...] = jnp.zeros_like(sums)

    def add(number, carry):
        wanted = asked[number]

        @pl.when(wanted >= 0)
        def _():
            source = number % slabs
            sums[source * blocks + wanted] += returned[number // slabs, source].astype(f32)

        return carry

    lax.fori_loop(0, LANES * slabs, add, 0)
    total = jnp.zeros((2, PAIR, panel.shape[1]), f32)
    for lane in range(LANES):
        total += returned[lane, slabs : slabs + 2].astype(f32)
    panel[...] = total.reshape(panel.shape)

    def spread(number, carry):
        position = global_pos[number]
        owner = position // tokens
        row = position % tokens

        @pl.when(owner % LANES == me)
        def _():
            to = owner // LANES * blocks + row // BLOCK
            for half in range(2):
                line = panel[pl.ds(number + half * GLOBALS, 1), :]
                sums[to, pl.ds(row % BLOCK + half * BLOCK, 1), :] += line

        return carry

    lax.fori_loop(0, GLOBALS, spread, 0)
    right_slab = jnp.where(me == LANES - 1, slab - 1, slab)
    left_slab = jnp.where(me == 0, slab + 1, slab)

    @pl.when(right_slab >= 0)
    def _():
        lane = (me + 1) % LANES
        sums[right_slab * blocks + blocks - 1] += returned[lane, slabs + 2].astype(f32)

    @pl.when(left_slab < slabs)
    def _():
        lane = (me + LANES - 1) % LANES
        sums[left_slab * blocks] += returned[lane, slabs + 2].astype(f32)

    def write(number, carry):
        lane_grads[number // blocks, number % blocks] = sums[number].astype(lane_grads.dtype)
        return carry

    lax.fori_loop(0, slabs * blocks, write, 0)


def shards(queries, key_states, value_states, out_weight, output_grad, rand_blocks, global_pos):
    bf16, f32 = jnp.bfloat16, jnp.float32
    tokens, columns = queries.shape
    blocks = tokens // BLOCK
    slabs = lax.axis_size("slab")
    slab, me = lax.axis_index("slab"), lax.axis_index("lane")
    smem, vmem = whole(pltpu.SMEM), whole()
    where = jnp.stack([me, slab]).astype(jnp.int32)
    slots = slabs + 3

    names = rand_blocks.reshape(-1)
    owner = names // blocks
    index = jnp.arange(LANES)[:, None] + LANES * jnp.arange(slabs)[None, :]
    hit = owner[None, None, :] == index[:, :, None]
    wanted = jnp.max(jnp.where(hit, (names % blocks)[None, None, :], -1), axis=-1)
    asked = lax.all_to_all(wanted, "lane", split_axis=0, concat_axis=0, tiled=True).reshape(-1)

    own = jnp.concatenate(
        [key_states.reshape(blocks, BLOCK, columns), value_states.reshape(blocks, BLOCK, columns)],
        axis=1,
    )
    lane_blocks = lax.all_gather(own, "slab", axis=0, tiled=False)

    lane_blocks, late_grad = lax.optimization_barrier((lane_blocks, output_grad))
    partial_grad = lax.dot_general(
        late_grad, out_weight, (((1,), (1,)), ((), ())), preferred_element_type=f32
    )
    grad_att = lax.psum_scatter(partial_grad, "head", scatter_dimension=1, tiled=True).astype(bf16)

    served = call(
        serve_kernel,
        shape((LANES, slots, PAIR, columns), bf16),
        [smem, smem, smem, vmem],
        [pltpu.VMEM((2 * GLOBALS, columns), f32)],
        moved=10 << 20,
    )(where, asked, global_pos, lane_blocks)
    arrived = lax.all_to_all(served, "lane", split_axis=0, concat_axis=0, tiled=True)

    padded = tokens + PAIR
    attended, query_grad, key_part, value_part, sent = call(
        attention_kernel,
        (
            shape((tokens, columns), bf16),
            shape((tokens, columns), bf16),
            shape((padded, columns), f32),
            shape((padded, columns), f32),
            shape((LANES, slots, PAIR, columns), bf16),
        ),
        [smem, smem] + [vmem] * 5,
        [
            pltpu.VMEM((padded, columns), bf16),
            pltpu.VMEM((padded, columns), bf16),
            pltpu.VMEM((2, GLOBALS, columns), bf16),
            pltpu.VMEM((2, GLOBALS, columns), f32),
        ],
        flops=1 << 30,
        moved=12 << 20,
    )(where, names, queries, grad_att, key_states, value_states, arrived)
    returned = lax.all_to_all(sent, "lane", split_axis=0, concat_axis=0, tiled=True)

    everywhere = lax.all_gather(attended, "head", axis=1, tiled=True)
    projected = jnp.dot(everywhere, out_weight, preferred_element_type=f32).astype(bf16)
    weight_part = lax.dot_general(
        everywhere, output_grad, (((0,), (0,)), ((), ())), preferred_element_type=f32
    ) * (1.0 / math.sqrt(tokens * slabs * LANES))
    features = weight_part.shape[1]
    weight_part = weight_part.reshape(slabs, LANES, -1, features).transpose(1, 0, 2, 3)
    weight_part = lax.all_to_all(weight_part, "lane", split_axis=0, concat_axis=0, tiled=True)
    weight_part = jnp.sum(weight_part, axis=0)
    weight_part = lax.all_to_all(weight_part, "slab", split_axis=0, concat_axis=0, tiled=True)
    weight_part = jnp.sum(weight_part, axis=0)
    weight_grad = lax.all_gather(weight_part, ("slab", "lane"), axis=0, tiled=True)

    lane_grads = call(
        collect_kernel,
        shape((slabs, blocks, PAIR, columns), bf16),
        [smem, smem, smem, vmem],
        [
            pltpu.VMEM((slabs * blocks, PAIR, columns), f32),
            pltpu.VMEM((2 * GLOBALS, columns), f32),
        ],
        moved=10 << 20,
    )(where, asked, global_pos, returned)
    others = lax.psum_scatter(lane_grads, "slab", scatter_dimension=0, tiled=False).astype(f32)
    key_grad = key_part[BLOCK:-BLOCK] + others[:, :BLOCK].reshape(tokens, columns)
    value_grad = value_part[BLOCK:-BLOCK] + others[:, BLOCK:].reshape(tokens, columns)
    return projected, query_grad, key_grad.astype(bf16), value_grad.astype(bf16), weight_grad


def solution(mesh):
    seq_count, head_count = mesh.devices.shape
    fine = Mesh(
        mesh.devices.reshape(seq_count // LANES, LANES, head_count), ("slab", "lane", "head")
    )
    seq = ("slab", "lane")
    placed = (
        P(seq, "head"),
        P(seq, "head"),
        P(seq, "head"),
        P(None, "head"),
        P(seq, "head"),
        P(seq, None),
        P(),
    )
    return jax.shard_map(
        shards,
        mesh=fine,
        in_specs=placed,
        out_specs=(
            P(seq, "head"),
            P(seq, "head"),
            P(seq, "head"),
            P(seq, "head"),
            P(None, "head"),
        ),
        check_vma=False,
    )
```

```python
import math

import jax
import jax.numpy as jnp
from jax import lax
from jax.experimental import pallas as pl
from jax.experimental.pallas import tpu as pltpu
from jax.sharding import Mesh
from jax.sharding import PartitionSpec as P

HEAD_DIM = 64
GLOBALS = 128
BLOCK = 64
EXTRA = GLOBALS // BLOCK + 1
R = 3
LANES = 8
TILE = 16
VMEM_LIMIT = 40 * 1024 * 1024


def whole(space=pltpu.VMEM):
    return pl.BlockSpec(memory_space=space)


def shape(dims, dtype):
    return jax.ShapeDtypeStruct(dims, dtype)


def call(kernel, out_shape, in_specs, scratch=(), flops=0, moved=0):
    return pl.pallas_call(
        kernel,
        out_shape=out_shape,
        in_specs=in_specs,
        out_specs=jax.tree.map(lambda _: whole(), out_shape),
        scratch_shapes=list(scratch),
        compiler_params=pltpu.CompilerParams(vmem_limit_bytes=VMEM_LIMIT),
        cost_estimate=pl.CostEstimate(flops=flops, bytes_accessed=moved, transcendentals=0),
    )


def serve_kernel(where, asked, global_pos, lane_blocks, send, panel):
    me, slab = where[0], where[1]
    slabs, blocks = lane_blocks.shape[:2]
    columns = panel.shape[1]
    tokens = blocks * BLOCK

    def serve(number, carry):
        source = number % slabs
        send[number // slabs, source] = lane_blocks[source, jnp.maximum(asked[number], 0)]
        return carry

    lax.fori_loop(0, LANES * slabs, serve, 0)

    panel[...] = jnp.zeros_like(panel)
    row_number = lax.broadcasted_iota(jnp.int32, (TILE, columns), 0)

    def pick(number, carry):
        position = global_pos[number]
        owner = position // tokens
        row = position % tokens

        @pl.when(owner % LANES == me)
        def _():
            inside = row % BLOCK
            first = pl.multiple_of(inside // TILE * TILE, TILE)
            rows = lane_blocks[owner // LANES, row // BLOCK, pl.ds(first, TILE), :]
            hit = row_number == inside % TILE
            panel[pl.ds(number, 1), :] = jnp.sum(
                jnp.where(hit, rows.astype(jnp.float32), 0.0), axis=0, keepdims=True
            )

        return carry

    lax.fori_loop(0, GLOBALS, pick, 0)
    panel_rows = panel[...].astype(send.dtype).reshape(EXTRA - 1, BLOCK, columns)

    def rest(to, carry):
        send[to, slabs : slabs + EXTRA - 1] = panel_rows
        to_right = to == (me + 1) % LANES
        source = jnp.where(
            to_right,
            jnp.where(me == LANES - 1, slab - 1, slab),
            jnp.where(me == 0, slab + 1, slab),
        )
        source = jnp.clip(source, 0, slabs - 1)
        send[to, slabs + EXTRA - 1] = lane_blocks[source, jnp.where(to_right, blocks - 1, 0)]
        return carry

    lax.fori_loop(0, LANES, rest, 0)


def attention_kernel(
    where,
    names,
    q,
    g,
    key,
    value,
    keys_arrived,
    values_arrived,
    attended,
    query_grad,
    key_grad,
    value_grad,
    send_keys,
    send_values,
    key_pad,
    value_pad,
    panel,
    panel_grad,
):
    me, slab = where[0], where[1]
    slabs = keys_arrived.shape[1] - EXTRA
    edge = slabs + EXTRA - 1
    tokens, columns = q.shape
    blocks = tokens // BLOCK
    scale = 1.0 / math.sqrt(HEAD_DIM)
    f32, bf16 = jnp.float32, jnp.bfloat16
    left_lane, right_lane = (me + LANES - 1) % LANES, (me + 1) % LANES
    key_pad[:BLOCK, :] = keys_arrived[left_lane, edge]
    value_pad[:BLOCK, :] = values_arrived[left_lane, edge]
    key_pad[BLOCK : BLOCK + tokens, :] = key[...]
    value_pad[BLOCK : BLOCK + tokens, :] = value[...]
    key_pad[BLOCK + tokens :, :] = keys_arrived[right_lane, edge]
    value_pad[BLOCK + tokens :, :] = values_arrived[right_lane, edge]
    for half, arrived in enumerate((keys_arrived, values_arrived)):
        panel_sum = jnp.zeros((EXTRA - 1, BLOCK, columns), f32)
        for lane in range(LANES):
            panel_sum += arrived[lane, slabs:edge].astype(f32)
        panel[half] = panel_sum.reshape(GLOBALS, columns).astype(bf16)
    key_grad[...] = jnp.zeros_like(key_grad)
    value_grad[...] = jnp.zeros_like(value_grad)
    panel_grad[...] = jnp.zeros_like(panel_grad)
    first_block = (slab * LANES + me) * blocks
    last_block = slabs * LANES * blocks - 1
    first_head = lax.broadcasted_iota(jnp.int32, (BLOCK, columns), 1) < HEAD_DIM
    window = 3 * BLOCK
    keys = window + GLOBALS + R * BLOCK
    key_column = lax.broadcasted_iota(jnp.int32, (1, keys), 1)

    def by_head(rows):
        zero = jnp.zeros_like(rows)
        return jnp.concatenate(
            [jnp.where(first_head, rows, zero), jnp.where(first_head, zero, rows)], axis=0
        )

    def joined(pair):
        return jnp.where(first_head, pair[:BLOCK], pair[BLOCK:])

    def dot(a, b, dims):
        return lax.dot_general(a, b, (dims, ((), ())), preferred_element_type=f32)

    def one(block, carry):
        row = pl.multiple_of(block * BLOCK, BLOCK)
        here = pl.ds(row, BLOCK)
        around = pl.ds(row, window)
        owners = [names[block * R + j] // blocks for j in range(R)]
        slots = [(owner % LANES, owner // LANES) for owner in owners]
        kk = jnp.concatenate(
            [key_pad[around, :], panel[0]] + [keys_arrived[a, b] for a, b in slots], axis=0
        )
        vv = jnp.concatenate(
            [value_pad[around, :], panel[1]] + [values_arrived[a, b] for a, b in slots], axis=0
        )
        q2 = by_head(q[here, :])
        g2 = by_head(g[here, :])
        number = first_block + block
        dead = ((key_column < BLOCK) & (number == 0)) | (
            (key_column >= 2 * BLOCK) & (key_column < window) & (number == last_block)
        )
        scores = dot(q2, kk, ((1,), (1,))) * scale
        scores = jnp.where(dead, -jnp.inf, scores)
        top = jnp.max(scores, axis=-1, keepdims=True)
        raised = jnp.exp(scores - top)
        probs = raised * (1.0 / jnp.sum(raised, axis=-1, keepdims=True))
        probs_b = probs.astype(bf16)
        att = joined(dot(probs_b, vv, ((1,), (0,)))).astype(bf16)
        attended[here, :] = att
        att_f = att.astype(f32)
        delta = jnp.sum(
            g2.astype(f32) * jnp.concatenate([att_f, att_f], axis=0), axis=-1, keepdims=True
        )
        slope = (probs * (dot(g2, vv, ((1,), (1,))) - delta)).astype(bf16)
        query_grad[here, :] = (scale * joined(dot(slope, kk, ((1,), (0,))))).astype(bf16)
        dk = scale * dot(slope, q2, ((0,), (0,)))
        dv = dot(probs_b, g2, ((0,), (0,)))
        key_grad[around, :] += dk[:window]
        value_grad[around, :] += dv[:window]
        panel_grad[0] += dk[window : window + GLOBALS]
        panel_grad[1] += dv[window : window + GLOBALS]
        for j, (a, b) in enumerate(slots):
            first = window + GLOBALS + j * BLOCK
            send_keys[a, b] = dk[first : first + BLOCK].astype(bf16)
            send_values[a, b] = dv[first : first + BLOCK].astype(bf16)
        return carry

    lax.fori_loop(0, blocks, one, 0)
    for half, (send, grad) in enumerate(((send_keys, key_grad), (send_values, value_grad))):
        panel_rows = panel_grad[half].astype(bf16).reshape(EXTRA - 1, BLOCK, columns)
        for lane in range(LANES):
            send[lane, slabs:edge] = panel_rows
        send[left_lane, edge] = grad[:BLOCK, :].astype(bf16)
        send[right_lane, edge] = grad[BLOCK + tokens :, :].astype(bf16)


def collect_kernel(where, asked, global_pos, returned, lane_grads, sums, panel):
    me, slab = where[0], where[1]
    slabs, blocks = lane_grads.shape[:2]
    tokens = blocks * BLOCK
    f32 = jnp.float32
    sums[...] = jnp.zeros_like(sums)

    def add(number, carry):
        wanted = asked[number]

        @pl.when(wanted >= 0)
        def _():
            source = number % slabs
            sums[source * blocks + wanted] += returned[number // slabs, source].astype(f32)

        return carry

    lax.fori_loop(0, LANES * slabs, add, 0)
    edge = slabs + EXTRA - 1
    total = jnp.zeros((EXTRA - 1, BLOCK, panel.shape[1]), f32)
    for lane in range(LANES):
        total += returned[lane, slabs:edge].astype(f32)
    panel[...] = total.reshape(panel.shape)

    def spread(number, carry):
        position = global_pos[number]
        owner = position // tokens
        row = position % tokens

        @pl.when(owner % LANES == me)
        def _():
            to = owner // LANES * blocks + row // BLOCK
            sums[to, pl.ds(row % BLOCK, 1), :] += panel[pl.ds(number, 1), :]

        return carry

    lax.fori_loop(0, GLOBALS, spread, 0)
    right_slab = jnp.where(me == LANES - 1, slab - 1, slab)
    left_slab = jnp.where(me == 0, slab + 1, slab)

    @pl.when(right_slab >= 0)
    def _():
        lane = (me + 1) % LANES
        sums[right_slab * blocks + blocks - 1] += returned[lane, edge].astype(f32)

    @pl.when(left_slab < slabs)
    def _():
        lane = (me + LANES - 1) % LANES
        sums[left_slab * blocks] += returned[lane, edge].astype(f32)

    def write(number, carry):
        lane_grads[number // blocks, number % blocks] = sums[number].astype(lane_grads.dtype)
        return carry

    lax.fori_loop(0, slabs * blocks, write, 0)


def shards(queries, key_states, value_states, out_weight, output_grad, rand_blocks, global_pos):
    bf16, f32 = jnp.bfloat16, jnp.float32
    tokens, columns = queries.shape
    blocks = tokens // BLOCK
    slabs, heads = lax.axis_size("slab"), lax.axis_size("head")
    slab, me, head = lax.axis_index("slab"), lax.axis_index("lane"), lax.axis_index("head")
    smem, vmem = whole(pltpu.SMEM), whole()
    where = jnp.stack([me, slab]).astype(jnp.int32)
    slots = slabs + EXTRA
    run = (blocks, BLOCK, columns)

    lane_keys = lax.all_gather(key_states.reshape(run), "slab", axis=0, tiled=False)

    names = rand_blocks.reshape(-1)
    owner = names // blocks
    index = jnp.arange(LANES)[:, None] + LANES * jnp.arange(slabs)[None, :]
    hit = owner[None, None, :] == index[:, :, None]
    wanted = jnp.max(jnp.where(hit, (names % blocks)[None, None, :], -1), axis=-1)
    late_values, wanted = lax.optimization_barrier((value_states, wanted))
    lane_values = lax.all_gather(late_values.reshape(run), "slab", axis=0, tiled=False)
    asked = lax.all_to_all(wanted, "lane", split_axis=0, concat_axis=0, tiled=True).reshape(-1)

    partial_grad = lax.dot_general(
        output_grad, out_weight, (((1,), (1,)), ((), ())), preferred_element_type=f32
    )
    partial_grad = partial_grad.reshape(tokens, heads, columns).transpose(1, 0, 2)
    partial_grad = lax.all_to_all(partial_grad, "head", split_axis=0, concat_axis=0, tiled=True)
    grad_att = jnp.sum(partial_grad, axis=0).astype(bf16)
    lane_keys, grad_att, asked = lax.optimization_barrier((lane_keys, grad_att, asked))

    def serve(lane_blocks):
        served = call(
            serve_kernel,
            shape((LANES, slots, BLOCK, columns), bf16),
            [smem, smem, smem, vmem],
            [pltpu.VMEM((GLOBALS, columns), f32)],
            moved=5 << 20,
        )(where, asked, global_pos, lane_blocks)
        return lax.all_to_all(served, "lane", split_axis=0, concat_axis=0, tiled=True)

    keys_arrived = serve(lane_keys)
    lane_values, keys_arrived = lax.optimization_barrier((lane_values, keys_arrived))
    values_arrived = serve(lane_values)

    padded = tokens + 2 * BLOCK
    attended, query_grad, key_part, value_part, keys_sent, values_sent = call(
        attention_kernel,
        (
            shape((tokens, columns), bf16),
            shape((tokens, columns), bf16),
            shape((padded, columns), f32),
            shape((padded, columns), f32),
            shape((LANES, slots, BLOCK, columns), bf16),
            shape((LANES, slots, BLOCK, columns), bf16),
        ),
        [smem, smem] + [vmem] * 6,
        [
            pltpu.VMEM((padded, columns), bf16),
            pltpu.VMEM((padded, columns), bf16),
            pltpu.VMEM((2, GLOBALS, columns), bf16),
            pltpu.VMEM((2, GLOBALS, columns), f32),
        ],
        flops=1 << 30,
        moved=12 << 20,
    )(where, names, queries, grad_att, key_states, value_states, keys_arrived, values_arrived)

    keys_returned = lax.all_to_all(keys_sent, "lane", split_axis=0, concat_axis=0, tiled=True)

    pieces = [attended] + [
        lax.ppermute(attended, "head", [(i, (i + k) % heads) for i in range(heads)])
        for k in range(1, heads)
    ]
    everywhere = jnp.concatenate(pieces, axis=1)
    order = (head - jnp.arange(heads)) % heads
    weight_rows = out_weight.reshape(heads, columns, -1).at[order].get(mode="promise_in_bounds")
    weight_rows = weight_rows.reshape(out_weight.shape)
    weight_part = lax.dot_general(
        everywhere, output_grad, (((0,), (0,)), ((), ())), preferred_element_type=f32
    ) * (1.0 / math.sqrt(tokens * slabs * LANES))
    features = weight_part.shape[1]
    keys_returned, weight_part = lax.optimization_barrier((keys_returned, weight_part))

    def collect(returned):
        return call(
            collect_kernel,
            shape((slabs,) + run, bf16),
            [smem, smem, smem, vmem],
            [pltpu.VMEM((slabs * blocks, BLOCK, columns), f32), pltpu.VMEM((GLOBALS, columns), f32)],
            moved=5 << 20,
        )(where, asked, global_pos, returned)

    def sum_slabs(lane_grads):
        return lax.psum_scatter(lane_grads, "slab", scatter_dimension=0, tiled=False)

    lane_grads = collect(keys_returned)
    lane_grads, values_sent = lax.optimization_barrier((lane_grads, values_sent))
    key_others = sum_slabs(lane_grads)
    values_returned = lax.all_to_all(values_sent, "lane", split_axis=0, concat_axis=0, tiled=True)

    weight_part = weight_part.reshape(LANES, -1, features)
    weight_part = lax.all_to_all(weight_part, "lane", split_axis=0, concat_axis=0, tiled=True)
    weight_part = jnp.sum(weight_part, axis=0)
    values_returned, weight_part, key_others = lax.optimization_barrier(
        (values_returned, weight_part, key_others)
    )
    lane_grads = collect(values_returned)
    lane_grads, weight_part = lax.optimization_barrier((lane_grads, weight_part))
    value_others = sum_slabs(lane_grads)

    weight_part = weight_part.reshape(slabs, -1, features)
    weight_part = lax.all_to_all(weight_part, "slab", split_axis=0, concat_axis=0, tiled=True)
    weight_part = jnp.sum(weight_part, axis=0)
    for axis in ("slab", "lane"):
        weight_part = jnp.broadcast_to(weight_part, (lax.axis_size(axis),) + weight_part.shape)
        weight_part = lax.all_to_all(weight_part, axis, split_axis=0, concat_axis=0, tiled=True)
        weight_part = weight_part.reshape(-1, features)
    weight_part = weight_part.reshape(heads, columns, features)
    weight_grad = weight_part.at[order].get(mode="promise_in_bounds")

    projected = jnp.dot(everywhere, weight_rows, preferred_element_type=f32).astype(bf16)
    key_others = key_others.astype(f32).reshape(tokens, columns)
    value_others = value_others.astype(f32).reshape(tokens, columns)
    key_grad = (key_part[BLOCK:-BLOCK] + key_others).astype(bf16)
    value_grad = (value_part[BLOCK:-BLOCK] + value_others).astype(bf16)
    return (
        projected,
        query_grad,
        key_grad,
        value_grad,
        weight_grad.reshape(heads * columns, features),
    )


def solution(mesh):
    seq_count, head_count = mesh.devices.shape
    fine = Mesh(
        mesh.devices.reshape(seq_count // LANES, LANES, head_count), ("slab", "lane", "head")
    )
    seq = ("slab", "lane")
    placed = (
        P(seq, "head"),
        P(seq, "head"),
        P(seq, "head"),
        P(None, "head"),
        P(seq, "head"),
        P(seq, None),
        P(),
    )
    return jax.shard_map(
        shards,
        mesh=fine,
        in_specs=placed,
        out_specs=(
            P(seq, "head"),
            P(seq, "head"),
            P(seq, "head"),
            P(seq, "head"),
            P(None, "head"),
        ),
        check_vma=False,
    )
```

```python
import math

import jax
import jax.numpy as jnp
from jax import lax
from jax.experimental import pallas as pl
from jax.experimental.pallas import tpu as pltpu
from jax.sharding import Mesh
from jax.sharding import PartitionSpec as P

HEAD_DIM = 64
BLOCK = 64
PAIR = 2 * BLOCK
LANES = 16
R = 3
GLOBALS = 128
VMEM_LIMIT = 40 * 1024 * 1024


def whole(space=pltpu.VMEM):
    return pl.BlockSpec(memory_space=space)


def shape(dims, dtype):
    return jax.ShapeDtypeStruct(dims, dtype)


def call(kernel, out_shape, in_specs, scratch=(), flops=0, moved=0):
    return pl.pallas_call(
        kernel,
        out_shape=out_shape,
        in_specs=in_specs,
        out_specs=jax.tree.map(lambda _: whole(), out_shape),
        scratch_shapes=list(scratch),
        compiler_params=pltpu.CompilerParams(vmem_limit_bytes=VMEM_LIMIT),
        cost_estimate=pl.CostEstimate(flops=flops, bytes_accessed=moved, transcendentals=0),
    )


def panel_kernel(token_row, key, value, panel, key_wide, value_wide, panel_wide):
    tokens = key.shape[0]
    key_wide[...] = key[...].astype(jnp.float32)
    value_wide[...] = value[...].astype(jnp.float32)
    panel_wide[...] = jnp.zeros_like(panel_wide)

    def one(number, carry):
        row = token_row[number]

        @pl.when((row >= 0) & (row < tokens))
        def _():
            panel_wide[pl.ds(number, 1), :] = key_wide[pl.ds(row, 1), :]
            panel_wide[pl.ds(number + GLOBALS, 1), :] = value_wide[pl.ds(row, 1), :]

        return carry

    lax.fori_loop(0, GLOBALS, one, 0)
    panel[...] = panel_wide[...].astype(panel.dtype)


def serve_kernel(asked, lane_blocks, send):
    slabs = lane_blocks.shape[0]

    def serve(number, carry):
        source = number % slabs
        send[number // slabs, source] = lane_blocks[source, jnp.maximum(asked[number], 0)]
        return carry

    lax.fori_loop(0, LANES * slabs, serve, 0)


def attention_kernel(
    place,
    names,
    q,
    g,
    key,
    value,
    left,
    right,
    panel,
    arrived,
    attended,
    query_grad,
    key_grad,
    value_grad,
    panel_grad,
    rims,
    send,
    key_pad,
    value_pad,
):
    tokens, columns = q.shape
    blocks = tokens // BLOCK
    scale = 1.0 / math.sqrt(HEAD_DIM)
    f32, bf16 = jnp.float32, jnp.bfloat16
    key_pad[:BLOCK, :] = left[:BLOCK, :]
    value_pad[:BLOCK, :] = left[BLOCK:, :]
    key_pad[BLOCK : BLOCK + tokens, :] = key[...]
    value_pad[BLOCK : BLOCK + tokens, :] = value[...]
    key_pad[BLOCK + tokens :, :] = right[:BLOCK, :]
    value_pad[BLOCK + tokens :, :] = right[BLOCK:, :]
    key_grad[...] = jnp.zeros_like(key_grad)
    value_grad[...] = jnp.zeros_like(value_grad)
    panel_grad[...] = jnp.zeros_like(panel_grad)
    first_block, last_block = place[0], place[1]
    first_head = lax.broadcasted_iota(jnp.int32, (BLOCK, columns), 1) < HEAD_DIM
    window = 3 * BLOCK
    keys = window + GLOBALS + R * BLOCK
    key_column = lax.broadcasted_iota(jnp.int32, (1, keys), 1)

    def by_head(rows):
        zero = jnp.zeros_like(rows)
        return jnp.concatenate(
            [jnp.where(first_head, rows, zero), jnp.where(first_head, zero, rows)], axis=0
        )

    def joined(pair):
        return jnp.where(first_head, pair[:BLOCK], pair[BLOCK:])

    def dot(a, b, dims):
        return lax.dot_general(a, b, (dims, ((), ())), preferred_element_type=f32)

    def one(block, carry):
        row = pl.multiple_of(block * BLOCK, BLOCK)
        here = pl.ds(row, BLOCK)
        around = pl.ds(row, window)
        owners = [names[block * R + j] // blocks for j in range(R)]
        slots = [(owner % LANES, owner // LANES) for owner in owners]
        kk = jnp.concatenate(
            [key_pad[around, :], panel[:GLOBALS, :]] + [arrived[a, b, :BLOCK, :] for a, b in slots], axis=0
        )
        vv = jnp.concatenate(
            [value_pad[around, :], panel[GLOBALS:, :]] + [arrived[a, b, BLOCK:, :] for a, b in slots], axis=0
        )
        q2 = by_head(q[here, :])
        g2 = by_head(g[here, :])
        number = first_block + block
        dead = ((key_column < BLOCK) & (number == 0)) | (
            (key_column >= 2 * BLOCK) & (key_column < window) & (number == last_block)
        )
        scores = dot(q2, kk, ((1,), (1,))) * scale
        scores = jnp.where(dead, -jnp.inf, scores)
        top = jnp.max(scores, axis=-1, keepdims=True)
        raised = jnp.exp(scores - top)
        probs = raised * (1.0 / jnp.sum(raised, axis=-1, keepdims=True))
        probs_b = probs.astype(bf16)
        att = joined(dot(probs_b, vv, ((1,), (0,)))).astype(bf16)
        attended[here, :] = att
        att_f = att.astype(f32)
        delta = jnp.sum(
            g2.astype(f32) * jnp.concatenate([att_f, att_f], axis=0), axis=-1, keepdims=True
        )
        slope = (probs * (dot(g2, vv, ((1,), (1,))) - delta)).astype(bf16)
        query_grad[here, :] = (scale * joined(dot(slope, kk, ((1,), (0,))))).astype(bf16)
        dk = scale * dot(slope, q2, ((0,), (0,)))
        dv = dot(probs_b, g2, ((0,), (0,)))
        key_grad[around, :] += dk[:window]
        value_grad[around, :] += dv[:window]
        panel_grad[:GLOBALS, :] += dk[window : window + GLOBALS]
        panel_grad[GLOBALS:, :] += dv[window : window + GLOBALS]
        for j, (a, b) in enumerate(slots):
            first = window + GLOBALS + j * BLOCK
            send[a, b, :BLOCK, :] = dk[first : first + BLOCK].astype(bf16)
            send[a, b, BLOCK:, :] = dv[first : first + BLOCK].astype(bf16)
        return carry

    lax.fori_loop(0, blocks, one, 0)
    for side, rows in enumerate((pl.ds(0, BLOCK), pl.ds(BLOCK + tokens, BLOCK))):
        rims[side, :BLOCK, :] = key_grad[rows, :].astype(bf16)
        rims[side, BLOCK:, :] = value_grad[rows, :].astype(bf16)


def collect_kernel(asked, returned, lane_grads, sums):
    slabs, blocks = lane_grads.shape[:2]
    sums[...] = jnp.zeros_like(sums)

    def add(number, carry):
        wanted = asked[number]

        @pl.when(wanted >= 0)
        def _():
            source = number % slabs
            sums[source * blocks + wanted] += returned[number // slabs, source].astype(jnp.float32)

        return carry

    lax.fori_loop(0, LANES * slabs, add, 0)

    def write(number, carry):
        lane_grads[number // blocks, number % blocks] = sums[number].astype(lane_grads.dtype)
        return carry

    lax.fori_loop(0, slabs * blocks, write, 0)


def finish_kernel(
    token_row,
    key_grad,
    value_grad,
    from_left,
    from_right,
    panel_grad,
    others,
    key_out,
    value_out,
    key_sum,
    value_sum,
):
    tokens = key_out.shape[0]
    f32 = jnp.float32

    def own(block, carry):
        row = pl.multiple_of(block * BLOCK, BLOCK)
        here, padded = pl.ds(row, BLOCK), pl.ds(row + BLOCK, BLOCK)
        key_sum[here, :] = key_grad[padded, :] + others[block, :BLOCK, :].astype(f32)
        value_sum[here, :] = value_grad[padded, :] + others[block, BLOCK:, :].astype(f32)
        return carry

    lax.fori_loop(0, others.shape[0], own, 0)
    key_sum[:BLOCK, :] += from_left[:BLOCK, :].astype(f32)
    value_sum[:BLOCK, :] += from_left[BLOCK:, :].astype(f32)
    key_sum[tokens - BLOCK :, :] += from_right[:BLOCK, :].astype(f32)
    value_sum[tokens - BLOCK :, :] += from_right[BLOCK:, :].astype(f32)

    def add_row(number, carry):
        row = token_row[number]

        @pl.when((row >= 0) & (row < tokens))
        def _():
            key_sum[pl.ds(row, 1), :] += panel_grad[pl.ds(number, 1), :]
            value_sum[pl.ds(row, 1), :] += panel_grad[pl.ds(number + GLOBALS, 1), :]

        return carry

    lax.fori_loop(0, GLOBALS, add_row, 0)
    key_out[...] = key_sum[...].astype(key_out.dtype)
    value_out[...] = value_sum[...].astype(value_out.dtype)


def exchange(array, axis):
    return lax.all_to_all(array, axis, split_axis=0, concat_axis=0, tiled=True)


def total(array):
    return jnp.sum(array.astype(jnp.float32), axis=0).astype(array.dtype)


def sum_over_slabs_and_spread(share):
    share = total(exchange(jnp.broadcast_to(share, (lax.axis_size("slab"),) + share.shape), "slab"))
    return exchange(jnp.broadcast_to(share, (LANES,) + share.shape), "lane")


def shards(queries, key_states, value_states, out_weight, output_grad, rand_blocks, global_pos):
    bf16, f32 = jnp.bfloat16, jnp.float32
    tokens, columns = queries.shape
    blocks = tokens // BLOCK
    slabs, heads = lax.axis_size("slab"), lax.axis_size("head")
    slab, me, head = lax.axis_index("slab"), lax.axis_index("lane"), lax.axis_index("head")
    position, seq_count = slab * LANES + me, slabs * LANES
    smem, vmem = whole(pltpu.SMEM), whole()
    token_row = global_pos - position * tokens

    own = jnp.concatenate(
        [key_states.reshape(blocks, BLOCK, columns), value_states.reshape(blocks, BLOCK, columns)],
        axis=1,
    )
    lane_blocks = lax.all_gather(own, "slab", axis=0, tiled=False)

    names = rand_blocks.reshape(-1)
    owner = names // blocks
    index = jnp.arange(LANES)[:, None] + LANES * jnp.arange(slabs)[None, :]
    hit = owner[None, None, :] == index[:, :, None]
    wanted = jnp.max(jnp.where(hit, (names % blocks)[None, None, :], -1), axis=-1)
    asked = exchange(wanted, "lane").reshape(-1)

    seq = ("slab", "lane")
    forth = [(i, i + 1) for i in range(seq_count - 1)]
    back = [(i + 1, i) for i in range(seq_count - 1)]
    left = lax.ppermute(own[blocks - 1], seq, forth)
    right = lax.ppermute(own[0], seq, back)

    panel = call(
        panel_kernel,
        shape((2 * GLOBALS, columns), bf16),
        [smem, vmem, vmem],
        [pltpu.VMEM((tokens, columns), f32)] * 2 + [pltpu.VMEM((2 * GLOBALS, columns), f32)],
        moved=1 << 20,
    )(token_row, key_states, value_states)
    panel = total(exchange(panel.reshape(LANES, -1, columns), "lane"))
    panel = sum_over_slabs_and_spread(panel).reshape(2 * GLOBALS, columns)

    lane_blocks, asked, left, right, panel, late_grad = lax.optimization_barrier(
        (lane_blocks, asked, left, right, panel, output_grad)
    )
    partial_grad = lax.dot_general(
        late_grad, out_weight, (((1,), (1,)), ((), ())), preferred_element_type=f32
    )
    grad_att = lax.psum_scatter(partial_grad, "head", scatter_dimension=1, tiled=True).astype(bf16)

    served = call(
        serve_kernel, shape((LANES, slabs, PAIR, columns), bf16), [smem, vmem], moved=8 << 20
    )(asked, lane_blocks)
    arrived = exchange(served, "lane")

    place = jnp.stack([position * blocks, seq_count * blocks - 1]).astype(jnp.int32)
    padded = tokens + PAIR
    attended, query_grad, key_part, value_part, panel_part, rims, sent = call(
        attention_kernel,
        (
            shape((tokens, columns), bf16),
            shape((tokens, columns), bf16),
            shape((padded, columns), f32),
            shape((padded, columns), f32),
            shape((2 * GLOBALS, columns), f32),
            shape((2, PAIR, columns), bf16),
            shape((LANES, slabs, PAIR, columns), bf16),
        ),
        [smem, smem] + [vmem] * 8,
        [pltpu.VMEM((padded, columns), bf16)] * 2,
        flops=1 << 30,
        moved=12 << 20,
    )(place, names, queries, grad_att, key_states, value_states, left, right, panel, arrived)

    returned = exchange(sent, "lane")
    from_left = lax.ppermute(rims[1], seq, forth)
    from_right = lax.ppermute(rims[0], seq, back)

    pieces = [attended] + [
        lax.ppermute(attended, "head", [(i, (i + k) % heads) for i in range(heads)])
        for k in range(1, heads)
    ]
    everywhere = jnp.concatenate(pieces, axis=1)
    order = (head - jnp.arange(heads)) % heads
    weight_rows = out_weight.reshape(heads, columns, -1).at[order].get(mode="promise_in_bounds")
    weight_rows = weight_rows.reshape(out_weight.shape)
    weight_part = lax.dot_general(
        everywhere, output_grad, (((0,), (0,)), ((), ())), preferred_element_type=f32
    ) * (1.0 / math.sqrt(tokens * seq_count))
    features = weight_part.shape[1]
    returned, from_left, from_right, weight_part = lax.optimization_barrier(
        (returned, from_left, from_right, weight_part)
    )
    lane_grads = call(
        collect_kernel,
        shape((slabs, blocks, PAIR, columns), bf16),
        [smem, vmem],
        [pltpu.VMEM((slabs * blocks, PAIR, columns), f32)],
        moved=10 << 20,
    )(asked, returned)
    lane_grads, weight_part, panel_part = lax.optimization_barrier(
        (lane_grads, weight_part, panel_part)
    )
    others = lax.psum_scatter(lane_grads, "slab", scatter_dimension=0, tiled=False)

    parts = [weight_part[:, at : at + columns] for at in range(0, features, columns)]
    parts = [part.reshape(LANES, -1, columns) for part in parts + [panel_part]]
    share = total(exchange(jnp.concatenate(parts, axis=1), "lane"))
    sums = sum_over_slabs_and_spread(share).reshape(LANES, -1, columns)
    lane_rows = heads * columns // LANES
    weight_grad = jnp.concatenate(
        [
            sums[:, at : at + lane_rows].reshape(heads, columns, columns)
            for at in range(0, lane_rows * (features // columns), lane_rows)
        ],
        axis=2,
    )
    weight_grad = weight_grad.at[order].get(mode="promise_in_bounds")
    weight_grad = weight_grad.reshape(heads * columns, features)
    panel_grad = sums[:, lane_rows * (features // columns) :].reshape(2 * GLOBALS, columns)

    projected = jnp.dot(everywhere, weight_rows, preferred_element_type=f32).astype(bf16)
    key_grad, value_grad = call(
        finish_kernel,
        (shape((tokens, columns), bf16), shape((tokens, columns), bf16)),
        [smem] + [vmem] * 6,
        [pltpu.VMEM((tokens, columns), f32)] * 2,
        moved=2 << 20,
    )(token_row, key_part, value_part, from_left, from_right, panel_grad, others)
    return projected, query_grad, key_grad, value_grad, weight_grad


def solution(mesh):
    seq_count, head_count = mesh.devices.shape
    fine = Mesh(
        mesh.devices.reshape(seq_count // LANES, LANES, head_count), ("slab", "lane", "head")
    )
    seq = ("slab", "lane")
    placed = (
        P(seq, "head"),
        P(seq, "head"),
        P(seq, "head"),
        P(None, "head"),
        P(seq, "head"),
        P(seq, None),
        P(),
    )
    return jax.shard_map(
        shards,
        mesh=fine,
        in_specs=placed,
        out_specs=(
            P(seq, "head"),
            P(seq, "head"),
            P(seq, "head"),
            P(seq, "head"),
            P(None, "head"),
        ),
        check_vma=False,
    )
```

```python
import math

import jax
import jax.numpy as jnp
from jax import lax
from jax.experimental import pallas as pl
from jax.experimental.pallas import tpu as pltpu
from jax.sharding import Mesh
from jax.sharding import PartitionSpec as P

HEAD_DIM = 64
BLOCK = 64
PAIR = 2 * BLOCK
LANES = 8
TILE = 16
PANEL = 2
FEW = 10
R = 3
GLOBALS = 128
VMEM_LIMIT = 40 * 1024 * 1024


def whole(space=pltpu.VMEM):
    return pl.BlockSpec(memory_space=space)


def shape(dims, dtype):
    return jax.ShapeDtypeStruct(dims, dtype)


def call(kernel, out_shape, in_specs, scratch=(), flops=0, moved=0):
    return pl.pallas_call(
        kernel,
        out_shape=out_shape,
        in_specs=in_specs,
        out_specs=jax.tree.map(lambda _: whole(), out_shape),
        scratch_shapes=list(scratch),
        compiler_params=pltpu.CompilerParams(vmem_limit_bytes=VMEM_LIMIT),
        cost_estimate=pl.CostEstimate(flops=flops, bytes_accessed=moved, transcendentals=0),
    )


def serve_kernel(where, asked, global_pos, lane_blocks, send, panel):
    me, blocks = where[0], where[1]
    tokens = blocks * BLOCK
    most = asked.shape[0] // LANES
    slots = send.shape[1] - PANEL

    def serve(number, carry):
        to = number // slots
        rank = number % slots
        send[to, rank] = lane_blocks[jnp.maximum(asked[to * most + rank], 0)]
        return carry

    lax.fori_loop(0, LANES * slots, serve, 0)

    panel[...] = jnp.zeros_like(panel)
    row_number = lax.broadcasted_iota(jnp.int32, (TILE, panel.shape[1]), 0)

    def pick(number, carry):
        position = global_pos[number]
        owner = position // tokens
        row = position % tokens

        @pl.when(owner % LANES == me)
        def _():
            source = owner // LANES * blocks + row // BLOCK
            inside = row % BLOCK
            first = pl.multiple_of(inside // TILE * TILE, TILE)
            hit = row_number == inside % TILE
            for half in range(2):
                rows = lane_blocks[source, pl.ds(first + half * BLOCK, TILE), :]
                panel[pl.ds(number + half * GLOBALS, 1), :] = jnp.sum(
                    jnp.where(hit, rows.astype(jnp.float32), 0.0), axis=0, keepdims=True
                )

        return carry

    lax.fori_loop(0, GLOBALS, pick, 0)
    panel_rows = panel[...].astype(send.dtype).reshape(PANEL, PAIR, panel.shape[1])
    for to in range(LANES):
        send[to, slots:] = panel_rows


def attention_kernel(
    place,
    names,
    ranks,
    q,
    g,
    key,
    value,
    left,
    right,
    arrived,
    attended,
    query_grad,
    key_grad,
    value_grad,
    rims,
    send,
    key_pad,
    value_pad,
    panel,
    panel_grad,
):
    tokens, columns = q.shape
    blocks = tokens // BLOCK
    scale = 1.0 / math.sqrt(HEAD_DIM)
    f32, bf16 = jnp.float32, jnp.bfloat16
    key_pad[:BLOCK, :] = left[:BLOCK, :]
    value_pad[:BLOCK, :] = left[BLOCK:, :]
    key_pad[BLOCK : BLOCK + tokens, :] = key[...]
    value_pad[BLOCK : BLOCK + tokens, :] = value[...]
    key_pad[BLOCK + tokens :, :] = right[:BLOCK, :]
    value_pad[BLOCK + tokens :, :] = right[BLOCK:, :]
    slots = arrived.shape[1] - PANEL
    panel_sum = jnp.zeros((PANEL, PAIR, columns), f32)
    for lane in range(LANES):
        panel_sum += arrived[lane, slots:].astype(f32)
    panel[...] = panel_sum.reshape(panel.shape).astype(bf16)
    key_grad[...] = jnp.zeros_like(key_grad)
    value_grad[...] = jnp.zeros_like(value_grad)
    panel_grad[...] = jnp.zeros_like(panel_grad)
    first_block, last_block = place[0], place[1]
    first_head = lax.broadcasted_iota(jnp.int32, (BLOCK, columns), 1) < HEAD_DIM
    window = 3 * BLOCK
    keys = window + GLOBALS + R * BLOCK
    key_column = lax.broadcasted_iota(jnp.int32, (1, keys), 1)

    def by_head(rows):
        zero = jnp.zeros_like(rows)
        return jnp.concatenate(
            [jnp.where(first_head, rows, zero), jnp.where(first_head, zero, rows)], axis=0
        )

    def joined(pair):
        return jnp.where(first_head, pair[:BLOCK], pair[BLOCK:])

    def dot(a, b, dims):
        return lax.dot_general(a, b, (dims, ((), ())), preferred_element_type=f32)

    def one(block, carry):
        row = pl.multiple_of(block * BLOCK, BLOCK)
        here = pl.ds(row, BLOCK)
        around = pl.ds(row, window)
        named = [block * R + j for j in range(R)]
        places = [(names[n] // blocks % LANES, ranks[n]) for n in named]
        kk = jnp.concatenate(
            [key_pad[around, :], panel[:GLOBALS, :]] + [arrived[a, b, :BLOCK, :] for a, b in places], axis=0
        )
        vv = jnp.concatenate(
            [value_pad[around, :], panel[GLOBALS:, :]] + [arrived[a, b, BLOCK:, :] for a, b in places], axis=0
        )
        q2 = by_head(q[here, :])
        g2 = by_head(g[here, :])
        number = first_block + block
        dead = ((key_column < BLOCK) & (number == 0)) | (
            (key_column >= 2 * BLOCK) & (key_column < window) & (number == last_block)
        )
        scores = dot(q2, kk, ((1,), (1,))) * scale
        scores = jnp.where(dead, -jnp.inf, scores)
        top = jnp.max(scores, axis=-1, keepdims=True)
        raised = jnp.exp(scores - top)
        probs = raised * (1.0 / jnp.sum(raised, axis=-1, keepdims=True))
        probs_b = probs.astype(bf16)
        att = joined(dot(probs_b, vv, ((1,), (0,)))).astype(bf16)
        attended[here, :] = att
        att_f = att.astype(f32)
        delta = jnp.sum(
            g2.astype(f32) * jnp.concatenate([att_f, att_f], axis=0), axis=-1, keepdims=True
        )
        slope = (probs * (dot(g2, vv, ((1,), (1,))) - delta)).astype(bf16)
        query_grad[here, :] = (scale * joined(dot(slope, kk, ((1,), (0,))))).astype(bf16)
        dk = scale * dot(slope, q2, ((0,), (0,)))
        dv = dot(probs_b, g2, ((0,), (0,)))
        key_grad[around, :] += dk[:window]
        value_grad[around, :] += dv[:window]
        panel_grad[:GLOBALS, :] += dk[window : window + GLOBALS]
        panel_grad[GLOBALS:, :] += dv[window : window + GLOBALS]
        for j, (a, b) in enumerate(places):
            first = window + GLOBALS + j * BLOCK
            send[a, b, :BLOCK, :] = dk[first : first + BLOCK].astype(bf16)
            send[a, b, BLOCK:, :] = dv[first : first + BLOCK].astype(bf16)
        return carry

    lax.fori_loop(0, blocks, one, 0)
    for side, rows in enumerate((pl.ds(0, BLOCK), pl.ds(BLOCK + tokens, BLOCK))):
        rims[side, :BLOCK, :] = key_grad[rows, :].astype(bf16)
        rims[side, BLOCK:, :] = value_grad[rows, :].astype(bf16)
    panel_rows = panel_grad[...].astype(bf16).reshape(PANEL, PAIR, columns)
    for lane in range(LANES):
        send[lane, slots:] = panel_rows


def collect_kernel(where, asked, global_pos, returned, lane_grads, sums, panel):
    me, blocks = where[0], where[1]
    tokens = blocks * BLOCK
    most = asked.shape[0] // LANES
    slots = returned.shape[1] - PANEL
    f32 = jnp.float32
    sums[...] = jnp.zeros_like(sums)

    def add(number, carry):
        source = number // slots
        rank = number % slots
        wanted = asked[source * most + rank]

        @pl.when(wanted >= 0)
        def _():
            sums[wanted] += returned[source, rank].astype(f32)

        return carry

    lax.fori_loop(0, LANES * slots, add, 0)
    total_rows = jnp.zeros((PANEL, PAIR, panel.shape[1]), f32)
    for lane in range(LANES):
        total_rows += returned[lane, slots:].astype(f32)
    panel[...] = total_rows.reshape(panel.shape)

    def spread(number, carry):
        position = global_pos[number]
        owner = position // tokens
        row = position % tokens

        @pl.when(owner % LANES == me)
        def _():
            to = owner // LANES * blocks + row // BLOCK
            for half in range(2):
                sums[to, pl.ds(row % BLOCK + half * BLOCK, 1), :] += panel[
                    pl.ds(number + half * GLOBALS, 1), :
                ]

        return carry

    lax.fori_loop(0, GLOBALS, spread, 0)

    def write(number, carry):
        lane_grads[number] = sums[number].astype(lane_grads.dtype)
        return carry

    lax.fori_loop(0, lane_grads.shape[0], write, 0)


def finish_kernel(
    key_grad,
    value_grad,
    from_left,
    from_right,
    others,
    key_out,
    value_out,
    key_sum,
    value_sum,
):
    tokens = key_out.shape[0]
    f32 = jnp.float32

    def own(block, carry):
        row = pl.multiple_of(block * BLOCK, BLOCK)
        here, padded = pl.ds(row, BLOCK), pl.ds(row + BLOCK, BLOCK)
        key_sum[here, :] = key_grad[padded, :] + others[block, :BLOCK, :].astype(f32)
        value_sum[here, :] = value_grad[padded, :] + others[block, BLOCK:, :].astype(f32)
        return carry

    lax.fori_loop(0, others.shape[0], own, 0)
    key_sum[:BLOCK, :] += from_left[:BLOCK, :].astype(f32)
    value_sum[:BLOCK, :] += from_left[BLOCK:, :].astype(f32)
    key_sum[tokens - BLOCK :, :] += from_right[:BLOCK, :].astype(f32)
    value_sum[tokens - BLOCK :, :] += from_right[BLOCK:, :].astype(f32)

    key_out[...] = key_sum[...].astype(key_out.dtype)
    value_out[...] = value_sum[...].astype(value_out.dtype)


def exchange(array, axis):
    return lax.all_to_all(array, axis, split_axis=0, concat_axis=0, tiled=True)


def spread(array, axis):
    return exchange(jnp.broadcast_to(array, (lax.axis_size(axis),) + array.shape), axis)


def shards(queries, key_states, value_states, out_weight, output_grad, rand_blocks, global_pos):
    bf16, f32 = jnp.bfloat16, jnp.float32
    tokens, columns = queries.shape
    blocks = tokens // BLOCK
    slabs, heads = lax.axis_size("slab"), lax.axis_size("head")
    slab, me, head = lax.axis_index("slab"), lax.axis_index("lane"), lax.axis_index("head")
    position, seq_count = slab * LANES + me, slabs * LANES
    smem, vmem = whole(pltpu.SMEM), whole()
    where = jnp.stack([me, jnp.int32(blocks)]).astype(jnp.int32)

    own = jnp.concatenate(
        [key_states.reshape(blocks, BLOCK, columns), value_states.reshape(blocks, BLOCK, columns)],
        axis=1,
    )
    lane_blocks = lax.all_gather(own, "slab", axis=0, tiled=True)

    names = rand_blocks.reshape(-1)
    owner = names // blocks
    lane, code = owner % LANES, owner // LANES * blocks + names % blocks
    number = jnp.arange(names.shape[0])
    same = (lane[:, None] == lane[None, :]) & (number[None, :] < number[:, None])
    ranks = jnp.sum(same.astype(jnp.int32), axis=1)
    index = jnp.arange(LANES * slabs)
    hit = (lane * slabs + ranks)[None, :] == index[:, None]
    wanted = jnp.max(jnp.where(hit, code[None, :], -1), axis=1).reshape(LANES, slabs)
    load = jnp.broadcast_to(jnp.max(ranks) + 1, (LANES, 1))
    heard = exchange(jnp.concatenate([wanted, load], axis=1), "lane")
    asked = heard[:, :slabs].reshape(-1)
    load = jnp.max(spread(jnp.max(heard[:, slabs:]).reshape(1), "slab"))

    partial_grad = lax.dot_general(
        output_grad, out_weight, (((1,), (1,)), ((), ())), preferred_element_type=f32
    )
    partial_grad = partial_grad.reshape(tokens, heads, columns).transpose(1, 0, 2)
    grad_att = jnp.sum(exchange(partial_grad, "head"), axis=0).astype(bf16)

    seq = ("slab", "lane")
    forth = [(i, i + 1) for i in range(seq_count - 1)]
    back = [(i + 1, i) for i in range(seq_count - 1)]
    left = lax.ppermute(own[blocks - 1], seq, forth)
    right = lax.ppermute(own[0], seq, back)

    order = (head - jnp.arange(heads)) % heads
    weight_rows = out_weight.reshape(heads, columns, -1).at[order].get(mode="promise_in_bounds")
    weight_rows = weight_rows.reshape(out_weight.shape)
    lane_blocks, asked, load, grad_att, left, right, weight_rows = lax.optimization_barrier(
        (lane_blocks, asked, load, grad_att, left, right, weight_rows)
    )
    place = jnp.stack([position * blocks, seq_count * blocks - 1]).astype(jnp.int32)
    padded = tokens + PAIR

    def middle(slots):
        slots += PANEL
        served = call(
            serve_kernel,
            shape((LANES, slots, PAIR, columns), bf16),
            [smem, smem, smem, vmem],
            [pltpu.VMEM((2 * GLOBALS, columns), f32)],
            moved=8 << 20,
        )(where, asked, global_pos, lane_blocks)
        arrived = exchange(served, "lane")
        attended, query_grad, key_part, value_part, rims, sent = call(
            attention_kernel,
            (
                shape((tokens, columns), bf16),
                shape((tokens, columns), bf16),
                shape((padded, columns), f32),
                shape((padded, columns), f32),
                shape((2, PAIR, columns), bf16),
                shape((LANES, slots, PAIR, columns), bf16),
            ),
            [smem, smem, smem] + [vmem] * 7,
            [pltpu.VMEM((padded, columns), bf16)] * 2
            + [
                pltpu.VMEM((2 * GLOBALS, columns), bf16),
                pltpu.VMEM((2 * GLOBALS, columns), f32),
            ],
            flops=1 << 30,
            moved=12 << 20,
        )(place, names, ranks, queries, grad_att, key_states, value_states, left, right, arrived)
        returned = exchange(sent, "lane")

        pieces = [attended] + [
            lax.ppermute(attended, "head", [(i, (i + k) % heads) for i in range(heads)])
            for k in range(1, heads)
        ]
        from_left = lax.ppermute(rims[1], seq, forth)
        from_right = lax.ppermute(rims[0], seq, back)
        everywhere = jnp.concatenate(pieces, axis=1)
        weight_part = lax.dot_general(
            everywhere, output_grad, (((0,), (0,)), ((), ())), preferred_element_type=f32
        ) * (1.0 / math.sqrt(tokens * seq_count))
        weight_part = weight_part.reshape(LANES, -1, weight_part.shape[1])
        step = LANES // 2
        while step:
            pair = weight_part.reshape((2, step) + weight_part.shape[1:])
            mine = me // step % 2
            kept = lax.dynamic_index_in_dim(pair, mine, 0, keepdims=False)
            other = lax.dynamic_index_in_dim(pair, 1 - mine, 0, keepdims=False)
            other = lax.ppermute(other, "lane", [(i, i ^ step) for i in range(LANES)])
            weight_part = kept + other
            step //= 2
        returned, from_left, from_right, weight_part = lax.optimization_barrier(
            (returned, from_left, from_right, weight_part)
        )
        lane_grads = call(
            collect_kernel,
            shape((slabs * blocks, PAIR, columns), bf16),
            [smem, smem, smem, vmem],
            [
                pltpu.VMEM((slabs * blocks, PAIR, columns), f32),
                pltpu.VMEM((2 * GLOBALS, columns), f32),
            ],
            moved=10 << 20,
        )(where, asked, global_pos, returned)
        return (
            everywhere,
            query_grad,
            key_part,
            value_part,
            from_left,
            from_right,
            weight_part,
            lane_grads,
        )

    few = lambda: middle(FEW)
    all_slots = lambda: middle(slabs)
    everywhere, query_grad, key_part, value_part, from_left, from_right, weight_part, lane_grads = (
        lax.cond(load <= FEW, few, all_slots) if FEW < slabs else all_slots()
    )
    others = lax.psum_scatter(lane_grads, "slab", scatter_dimension=0, tiled=True)

    features = weight_part.shape[-1]
    share = jnp.sum(exchange(weight_part.reshape(slabs, -1, features), "slab"), axis=0)
    share = spread(share, "slab").reshape(-1, features)
    weight_grad = spread(share, "lane").reshape(heads, columns, features)
    weight_grad = weight_grad.at[order].get(mode="promise_in_bounds")
    weight_grad = weight_grad.reshape(heads * columns, features)

    projected = jnp.dot(everywhere, weight_rows, preferred_element_type=f32).astype(bf16)
    key_grad, value_grad = call(
        finish_kernel,
        (shape((tokens, columns), bf16), shape((tokens, columns), bf16)),
        [vmem] * 5,
        [pltpu.VMEM((tokens, columns), f32)] * 2,
        moved=2 << 20,
    )(key_part, value_part, from_left, from_right, others)
    return projected, query_grad, key_grad, value_grad, weight_grad


def solution(mesh):
    seq_count, head_count = mesh.devices.shape
    fine = Mesh(
        mesh.devices.reshape(seq_count // LANES, LANES, head_count), ("slab", "lane", "head")
    )
    seq = ("slab", "lane")
    placed = (
        P(seq, "head"),
        P(seq, "head"),
        P(seq, "head"),
        P(None, "head"),
        P(seq, "head"),
        P(seq, None),
        P(),
    )
    return jax.shard_map(
        shards,
        mesh=fine,
        in_specs=placed,
        out_specs=(
            P(seq, "head"),
            P(seq, "head"),
            P(seq, "head"),
            P(seq, "head"),
            P(None, "head"),
        ),
        check_vma=False,
    )
```

```python
import math

import jax
import jax.numpy as jnp
from jax import lax
from jax.experimental import pallas as pl
from jax.experimental.pallas import tpu as pltpu
from jax.sharding import Mesh
from jax.sharding import PartitionSpec as P

HEAD_DIM = 64
BLOCK = 64
PAIR = 2 * BLOCK
LANES = 8
TILE = 16
FEW = 10
FEW_ROWS = 32
R = 3
GLOBALS = 128
VMEM_LIMIT = 40 * 1024 * 1024


def whole(space=pltpu.VMEM):
    return pl.BlockSpec(memory_space=space)


def shape(dims, dtype):
    return jax.ShapeDtypeStruct(dims, dtype)


def call(kernel, out_shape, in_specs, scratch=(), flops=0, moved=0):
    return pl.pallas_call(
        kernel,
        out_shape=out_shape,
        in_specs=in_specs,
        out_specs=jax.tree.map(lambda _: whole(), out_shape),
        scratch_shapes=list(scratch),
        compiler_params=pltpu.CompilerParams(vmem_limit_bytes=VMEM_LIMIT),
        cost_estimate=pl.CostEstimate(flops=flops, bytes_accessed=moved, transcendentals=0),
    )


def serve_kernel(where, asked, global_pos, global_rank, lane_blocks, send, panel):
    me, blocks = where[0], where[1]
    tokens = blocks * BLOCK
    most = asked.shape[0] // LANES
    room = panel.shape[0] // 2
    slots = send.shape[1] // PAIR if room < GLOBALS else most

    def serve(number, carry):
        to = number // slots
        rank = number % slots
        rows = pl.ds(pl.multiple_of(rank * PAIR, PAIR), PAIR)
        send[to, rows, :] = lane_blocks[jnp.maximum(asked[to * most + rank], 0)]
        return carry

    lax.fori_loop(0, LANES * slots, serve, 0)

    panel[...] = jnp.zeros_like(panel)
    row_number = lax.broadcasted_iota(jnp.int32, (TILE, panel.shape[1]), 0)

    def pick(number, carry):
        position = global_pos[number]
        owner = position // tokens
        row = position % tokens

        @pl.when(owner % LANES == me)
        def _():
            source = owner // LANES * blocks + row // BLOCK
            inside = row % BLOCK
            first = pl.multiple_of(inside // TILE * TILE, TILE)
            hit = row_number == inside % TILE
            for half in range(2):
                rows = lane_blocks[source, pl.ds(first + half * BLOCK, TILE), :]
                panel[pl.ds(global_rank[number] + half * room, 1), :] = jnp.sum(
                    jnp.where(hit, rows.astype(jnp.float32), 0.0), axis=0, keepdims=True
                )

        return carry

    lax.fori_loop(0, GLOBALS, pick, 0)
    panel_rows = panel[...].astype(send.dtype)
    for to in range(LANES):
        send[to, slots * PAIR :, :] = panel_rows


def attention_kernel(
    place,
    names,
    ranks,
    q,
    g,
    key,
    value,
    left,
    right,
    global_place,
    arrived,
    attended,
    query_grad,
    key_grad,
    value_grad,
    rims,
    send,
    key_pad,
    value_pad,
    panel,
    panel_grad,
):
    tokens, columns = q.shape
    blocks = tokens // BLOCK
    scale = 1.0 / math.sqrt(HEAD_DIM)
    f32, bf16 = jnp.float32, jnp.bfloat16
    key_pad[:BLOCK, :] = left[:BLOCK, :]
    value_pad[:BLOCK, :] = left[BLOCK:, :]
    key_pad[BLOCK : BLOCK + tokens, :] = key[...]
    value_pad[BLOCK : BLOCK + tokens, :] = value[...]
    key_pad[BLOCK + tokens :, :] = right[:BLOCK, :]
    value_pad[BLOCK + tokens :, :] = right[BLOCK:, :]
    key_grad[...] = jnp.zeros_like(key_grad)
    value_grad[...] = jnp.zeros_like(value_grad)
    panel_grad[...] = jnp.zeros_like(panel_grad)
    first_block, last_block = place[0], place[1]
    first_head = lax.broadcasted_iota(jnp.int32, (BLOCK, columns), 1) < HEAD_DIM
    window = 3 * BLOCK
    keys = window + GLOBALS + R * BLOCK
    key_column = lax.broadcasted_iota(jnp.int32, (1, keys), 1)

    def by_head(rows):
        zero = jnp.zeros_like(rows)
        return jnp.concatenate(
            [jnp.where(first_head, rows, zero), jnp.where(first_head, zero, rows)], axis=0
        )

    def joined(pair):
        return jnp.where(first_head, pair[:BLOCK], pair[BLOCK:])

    def dot(a, b, dims):
        return lax.dot_general(a, b, (dims, ((), ())), preferred_element_type=f32)

    room = GLOBALS if arrived.shape[1] % PAIR == 0 else arrived.shape[1] % PAIR // 2
    first_row = arrived.shape[1] - 2 * room
    packed = lax.broadcasted_iota(jnp.int32, (GLOBALS, LANES * room), 1)
    chosen = jnp.where(packed == global_place[...], 1.0, 0.0).astype(bf16)
    for half in range(2):
        begin = first_row + half * room
        rows = [arrived[lane, begin : begin + room, :] for lane in range(LANES)]
        panel[half * GLOBALS : (half + 1) * GLOBALS, :] = dot(
            chosen, jnp.concatenate(rows, axis=0), ((1,), (0,))
        ).astype(bf16)

    def one(block, carry):
        row = pl.multiple_of(block * BLOCK, BLOCK)
        here = pl.ds(row, BLOCK)
        around = pl.ds(row, window)
        named = [block * R + j for j in range(R)]
        places = [
            (names[n] // blocks % LANES, pl.multiple_of(ranks[n] * PAIR, PAIR)) for n in named
        ]
        kk = jnp.concatenate(
            [key_pad[around, :], panel[:GLOBALS, :]] + [arrived[a, pl.ds(b, BLOCK), :] for a, b in places], axis=0
        )
        vv = jnp.concatenate(
            [value_pad[around, :], panel[GLOBALS:, :]] + [arrived[a, pl.ds(b + BLOCK, BLOCK), :] for a, b in places], axis=0
        )
        q2 = by_head(q[here, :])
        g2 = by_head(g[here, :])
        number = first_block + block
        dead = ((key_column < BLOCK) & (number == 0)) | (
            (key_column >= 2 * BLOCK) & (key_column < window) & (number == last_block)
        )
        scores = dot(q2, kk, ((1,), (1,))) * scale
        scores = jnp.where(dead, -jnp.inf, scores)
        top = jnp.max(scores, axis=-1, keepdims=True)
        raised = jnp.exp(scores - top)
        probs = raised * (1.0 / jnp.sum(raised, axis=-1, keepdims=True))
        probs_b = probs.astype(bf16)
        att = joined(dot(probs_b, vv, ((1,), (0,)))).astype(bf16)
        attended[here, :] = att
        att_f = att.astype(f32)
        delta = jnp.sum(
            g2.astype(f32) * jnp.concatenate([att_f, att_f], axis=0), axis=-1, keepdims=True
        )
        slope = (probs * (dot(g2, vv, ((1,), (1,))) - delta)).astype(bf16)
        query_grad[here, :] = (scale * joined(dot(slope, kk, ((1,), (0,))))).astype(bf16)
        dk = scale * dot(slope, q2, ((0,), (0,)))
        dv = dot(probs_b, g2, ((0,), (0,)))
        key_grad[around, :] += dk[:window]
        value_grad[around, :] += dv[:window]
        panel_grad[:GLOBALS, :] += dk[window : window + GLOBALS]
        panel_grad[GLOBALS:, :] += dv[window : window + GLOBALS]
        for j, (a, b) in enumerate(places):
            first = window + GLOBALS + j * BLOCK
            send[a, pl.ds(b, BLOCK), :] = dk[first : first + BLOCK].astype(bf16)
            send[a, pl.ds(b + BLOCK, BLOCK), :] = dv[first : first + BLOCK].astype(bf16)
        return carry

    lax.fori_loop(0, blocks, one, 0)
    for side, rows in enumerate((pl.ds(0, BLOCK), pl.ds(BLOCK + tokens, BLOCK))):
        rims[side, :BLOCK, :] = key_grad[rows, :].astype(bf16)
        rims[side, BLOCK:, :] = value_grad[rows, :].astype(bf16)
    for half in range(2):
        begin = first_row + half * room
        rows = panel_grad[half * GLOBALS : (half + 1) * GLOBALS, :].astype(bf16)
        rows = dot(chosen, rows, ((0,), (0,))).astype(bf16)
        for lane in range(LANES):
            send[lane, begin : begin + room, :] = rows[lane * room : (lane + 1) * room]


def collect_kernel(where, asked, global_pos, global_rank, returned, lane_grads, sums, panel):
    me, blocks = where[0], where[1]
    tokens = blocks * BLOCK
    most = asked.shape[0] // LANES
    room = panel.shape[0] // 2
    slots = returned.shape[1] // PAIR if room < GLOBALS else most
    f32 = jnp.float32
    sums[...] = jnp.zeros_like(sums)

    def add(number, carry):
        source = number // slots
        rank = number % slots
        wanted = asked[source * most + rank]

        @pl.when(wanted >= 0)
        def _():
            rows = pl.ds(pl.multiple_of(rank * PAIR, PAIR), PAIR)
            sums[wanted] += returned[source, rows, :].astype(f32)

        return carry

    lax.fori_loop(0, LANES * slots, add, 0)
    total_rows = jnp.zeros(panel.shape, f32)
    for lane in range(LANES):
        total_rows += returned[lane, slots * PAIR :, :].astype(f32)
    panel[...] = total_rows

    def spread(number, carry):
        position = global_pos[number]
        owner = position // tokens
        row = position % tokens

        @pl.when(owner % LANES == me)
        def _():
            to = owner // LANES * blocks + row // BLOCK
            for half in range(2):
                sums[to, pl.ds(row % BLOCK + half * BLOCK, 1), :] += panel[
                    pl.ds(global_rank[number] + half * room, 1), :
                ]

        return carry

    lax.fori_loop(0, GLOBALS, spread, 0)

    def write(number, carry):
        lane_grads[number] = sums[number].astype(lane_grads.dtype)
        return carry

    lax.fori_loop(0, lane_grads.shape[0], write, 0)


def finish_kernel(
    key_grad,
    value_grad,
    from_left,
    from_right,
    others,
    key_out,
    value_out,
    key_sum,
    value_sum,
):
    tokens = key_out.shape[0]
    f32 = jnp.float32

    def own(block, carry):
        row = pl.multiple_of(block * BLOCK, BLOCK)
        here, padded = pl.ds(row, BLOCK), pl.ds(row + BLOCK, BLOCK)
        key_sum[here, :] = key_grad[padded, :] + others[block, :BLOCK, :].astype(f32)
        value_sum[here, :] = value_grad[padded, :] + others[block, BLOCK:, :].astype(f32)
        return carry

    lax.fori_loop(0, others.shape[0], own, 0)
    key_sum[:BLOCK, :] += from_left[:BLOCK, :].astype(f32)
    value_sum[:BLOCK, :] += from_left[BLOCK:, :].astype(f32)
    key_sum[tokens - BLOCK :, :] += from_right[:BLOCK, :].astype(f32)
    value_sum[tokens - BLOCK :, :] += from_right[BLOCK:, :].astype(f32)

    key_out[...] = key_sum[...].astype(key_out.dtype)
    value_out[...] = value_sum[...].astype(value_out.dtype)


def exchange(array, axis):
    return lax.all_to_all(array, axis, split_axis=0, concat_axis=0, tiled=True)


def spread(array, axis):
    return exchange(jnp.broadcast_to(array, (lax.axis_size(axis),) + array.shape), axis)


def shards(queries, key_states, value_states, out_weight, output_grad, rand_blocks, global_pos):
    bf16, f32 = jnp.bfloat16, jnp.float32
    tokens, columns = queries.shape
    blocks = tokens // BLOCK
    slabs, heads = lax.axis_size("slab"), lax.axis_size("head")
    slab, me, head = lax.axis_index("slab"), lax.axis_index("lane"), lax.axis_index("head")
    position, seq_count = slab * LANES + me, slabs * LANES
    smem, vmem = whole(pltpu.SMEM), whole()
    where = jnp.stack([me, jnp.int32(blocks)]).astype(jnp.int32)

    own = jnp.concatenate(
        [key_states.reshape(blocks, BLOCK, columns), value_states.reshape(blocks, BLOCK, columns)],
        axis=1,
    )
    lane_blocks = lax.all_gather(own, "slab", axis=0, tiled=True)

    names = rand_blocks.reshape(-1)
    owner = names // blocks
    lane, code = owner % LANES, owner // LANES * blocks + names % blocks
    number = jnp.arange(names.shape[0])
    same = (lane[:, None] == lane[None, :]) & (number[None, :] < number[:, None])
    ranks = jnp.sum(same.astype(jnp.int32), axis=1)
    index = jnp.arange(LANES * slabs)
    hit = (lane * slabs + ranks)[None, :] == index[:, None]
    wanted = jnp.max(jnp.where(hit, code[None, :], -1), axis=1).reshape(LANES, slabs)
    load = jnp.broadcast_to(jnp.max(ranks) + 1, (LANES, 1))
    global_lane = global_pos // tokens % LANES
    number = jnp.arange(GLOBALS)
    same = (global_lane[:, None] == global_lane[None, :]) & (number[None, :] < number[:, None])
    global_rank = jnp.sum(same.astype(jnp.int32), axis=1)
    heard = exchange(jnp.concatenate([wanted, load], axis=1), "lane")
    asked = heard[:, :slabs].reshape(-1)
    load = jnp.max(spread(jnp.max(heard[:, slabs:]).reshape(1), "slab"))
    fits = (load <= FEW) & (jnp.max(global_rank) < FEW_ROWS)

    partial_grad = lax.dot_general(
        output_grad, out_weight, (((1,), (1,)), ((), ())), preferred_element_type=f32
    )
    partial_grad = partial_grad.reshape(tokens, heads, columns).transpose(1, 0, 2)
    grad_att = jnp.sum(exchange(partial_grad, "head"), axis=0).astype(bf16)

    seq = ("slab", "lane")
    forth = [(i, i + 1) for i in range(seq_count - 1)]
    back = [(i + 1, i) for i in range(seq_count - 1)]
    left = lax.ppermute(own[blocks - 1], seq, forth)
    right = lax.ppermute(own[0], seq, back)

    order = (head - jnp.arange(heads)) % heads
    weight_rows = out_weight.reshape(heads, columns, -1).at[order].get(mode="promise_in_bounds")
    weight_rows = weight_rows.reshape(out_weight.shape)
    lane_blocks, asked, fits, grad_att, left, right, weight_rows = lax.optimization_barrier(
        (lane_blocks, asked, fits, grad_att, left, right, weight_rows)
    )
    place = jnp.stack([position * blocks, seq_count * blocks - 1]).astype(jnp.int32)
    padded = tokens + PAIR

    def middle(slots, room):
        sent_rows = slots * PAIR + 2 * room
        global_place = (global_lane * room + global_rank).reshape(GLOBALS, 1)
        served = call(
            serve_kernel,
            shape((LANES, sent_rows, columns), bf16),
            [smem, smem, smem, smem, vmem],
            [pltpu.VMEM((2 * room, columns), f32)],
            moved=8 << 20,
        )(where, asked, global_pos, global_rank, lane_blocks)
        arrived = exchange(served, "lane")
        attended, query_grad, key_part, value_part, rims, sent = call(
            attention_kernel,
            (
                shape((tokens, columns), bf16),
                shape((tokens, columns), bf16),
                shape((padded, columns), f32),
                shape((padded, columns), f32),
                shape((2, PAIR, columns), bf16),
                shape((LANES, sent_rows, columns), bf16),
            ),
            [smem, smem, smem] + [vmem] * 8,
            [pltpu.VMEM((padded, columns), bf16)] * 2
            + [
                pltpu.VMEM((2 * GLOBALS, columns), bf16),
                pltpu.VMEM((2 * GLOBALS, columns), f32),
            ],
            flops=1 << 30,
            moved=12 << 20,
        )(
            place,
            names,
            ranks,
            queries,
            grad_att,
            key_states,
            value_states,
            left,
            right,
            global_place,
            arrived,
        )
        returned = exchange(sent, "lane")

        pieces = [attended] + [
            lax.ppermute(attended, "head", [(i, (i + k) % heads) for i in range(heads)])
            for k in range(1, heads)
        ]
        from_left = lax.ppermute(rims[1], seq, forth)
        from_right = lax.ppermute(rims[0], seq, back)
        everywhere = jnp.concatenate(pieces, axis=1)
        weight_part = lax.dot_general(
            everywhere, output_grad, (((0,), (0,)), ((), ())), preferred_element_type=f32
        ) * (1.0 / math.sqrt(tokens * seq_count))
        returned, from_left, from_right, weight_part = lax.optimization_barrier(
            (returned, from_left, from_right, weight_part)
        )
        lane_grads = call(
            collect_kernel,
            shape((slabs * blocks, PAIR, columns), bf16),
            [smem, smem, smem, smem, vmem],
            [
                pltpu.VMEM((slabs * blocks, PAIR, columns), f32),
                pltpu.VMEM((2 * room, columns), f32),
            ],
            moved=10 << 20,
        )(where, asked, global_pos, global_rank, returned)
        return (
            everywhere,
            query_grad,
            key_part,
            value_part,
            from_left,
            from_right,
            weight_part,
            lane_grads,
        )

    few = lambda: middle(FEW, FEW_ROWS)
    all_slots = lambda: middle(slabs, GLOBALS)
    everywhere, query_grad, key_part, value_part, from_left, from_right, weight_part, lane_grads = (
        lax.cond(fits, few, all_slots) if FEW < slabs else all_slots()
    )
    others = lax.psum_scatter(lane_grads, "slab", scatter_dimension=0, tiled=True)

    weight_part = weight_part.reshape(LANES, -1, weight_part.shape[1])
    step = LANES // 2
    while step:
        pair = weight_part.reshape((2, step) + weight_part.shape[1:])
        mine = me // step % 2
        kept = lax.dynamic_index_in_dim(pair, mine, 0, keepdims=False)
        other = lax.dynamic_index_in_dim(pair, 1 - mine, 0, keepdims=False)
        other = lax.ppermute(other, "lane", [(i, i ^ step) for i in range(LANES)])
        weight_part = kept + other
        step //= 2
    features = weight_part.shape[-1]
    share = jnp.sum(exchange(weight_part.reshape(slabs, -1, features), "slab"), axis=0)
    share = spread(share, "slab").reshape(-1, features)
    weight_grad = spread(share, "lane").reshape(heads, columns, features)
    weight_grad = weight_grad.at[order].get(mode="promise_in_bounds")
    weight_grad = weight_grad.reshape(heads * columns, features)

    projected = jnp.dot(everywhere, weight_rows, preferred_element_type=f32).astype(bf16)
    key_grad, value_grad = call(
        finish_kernel,
        (shape((tokens, columns), bf16), shape((tokens, columns), bf16)),
        [vmem] * 5,
        [pltpu.VMEM((tokens, columns), f32)] * 2,
        moved=2 << 20,
    )(key_part, value_part, from_left, from_right, others)
    return projected, query_grad, key_grad, value_grad, weight_grad


def solution(mesh):
    seq_count, head_count = mesh.devices.shape
    fine = Mesh(
        mesh.devices.reshape(seq_count // LANES, LANES, head_count), ("slab", "lane", "head")
    )
    seq = ("slab", "lane")
    placed = (
        P(seq, "head"),
        P(seq, "head"),
        P(seq, "head"),
        P(None, "head"),
        P(seq, "head"),
        P(seq, None),
        P(),
    )
    return jax.shard_map(
        shards,
        mesh=fine,
        in_specs=placed,
        out_specs=(
            P(seq, "head"),
            P(seq, "head"),
            P(seq, "head"),
            P(seq, "head"),
            P(None, "head"),
        ),
        check_vma=False,
    )
```

```python
import math

import jax
import jax.numpy as jnp
from jax import lax
from jax.experimental import pallas as pl
from jax.experimental.pallas import tpu as pltpu
from jax.sharding import Mesh
from jax.sharding import PartitionSpec as P

HEAD_DIM = 64
BLOCK = 64
PAIR = 2 * BLOCK
LANES = 8
TILE = 16
FEW = 10
FEW_ROWS = 32
R = 3
GLOBALS = 128
VMEM_LIMIT = 40 * 1024 * 1024


def whole(space=pltpu.VMEM):
    return pl.BlockSpec(memory_space=space)


def shape(dims, dtype):
    return jax.ShapeDtypeStruct(dims, dtype)


def call(kernel, out_shape, in_specs, scratch=(), flops=0, moved=0):
    return pl.pallas_call(
        kernel,
        out_shape=out_shape,
        in_specs=in_specs,
        out_specs=jax.tree.map(lambda _: whole(), out_shape),
        scratch_shapes=list(scratch),
        compiler_params=pltpu.CompilerParams(vmem_limit_bytes=VMEM_LIMIT),
        cost_estimate=pl.CostEstimate(flops=flops, bytes_accessed=moved, transcendentals=0),
    )


def serve_kernel(asked, global_block, global_row, lane_blocks, send, panel):
    room = panel.shape[0] // 2
    most = asked.shape[0] // LANES
    slots = send.shape[1] // PAIR if room < GLOBALS else most
    for to in range(LANES):
        for rank in range(slots):
            wanted = jnp.maximum(asked[to * most + rank], 0)
            send[to, rank * PAIR : (rank + 1) * PAIR, :] = lane_blocks[wanted]

    panel[...] = jnp.zeros_like(panel)
    row_number = lax.broadcasted_iota(jnp.int32, (TILE, panel.shape[1]), 0)

    def pick(number, carry):
        source, inside = global_block[number], global_row[number]

        @pl.when(source >= 0)
        def _():
            first = pl.multiple_of(inside // TILE * TILE, TILE)
            hit = row_number == inside % TILE
            for half in range(2):
                rows = lane_blocks[source, pl.ds(first + half * BLOCK, TILE), :]
                panel[pl.ds(number + half * room, 1), :] = jnp.sum(
                    jnp.where(hit, rows.astype(jnp.float32), 0.0), axis=0, keepdims=True
                )

        return carry

    lax.fori_loop(0, room, pick, 0)
    panel_rows = panel[...].astype(send.dtype)
    for to in range(LANES):
        send[to, slots * PAIR :, :] = panel_rows


def attention_kernel(
    place,
    names,
    ranks,
    q,
    g,
    key,
    value,
    left,
    right,
    global_place,
    arrived,
    attended,
    query_grad,
    key_grad,
    value_grad,
    rims,
    send,
    key_pad,
    value_pad,
    panel,
    panel_grad,
):
    tokens, columns = q.shape
    blocks = tokens // BLOCK
    scale = 1.0 / math.sqrt(HEAD_DIM)
    f32, bf16 = jnp.float32, jnp.bfloat16
    key_pad[:BLOCK, :] = left[:BLOCK, :]
    value_pad[:BLOCK, :] = left[BLOCK:, :]
    key_pad[BLOCK : BLOCK + tokens, :] = key[...]
    value_pad[BLOCK : BLOCK + tokens, :] = value[...]
    key_pad[BLOCK + tokens :, :] = right[:BLOCK, :]
    value_pad[BLOCK + tokens :, :] = right[BLOCK:, :]
    key_grad[...] = jnp.zeros_like(key_grad)
    value_grad[...] = jnp.zeros_like(value_grad)
    panel_grad[...] = jnp.zeros_like(panel_grad)
    first_block, last_block = place[0], place[1]
    first_head = lax.broadcasted_iota(jnp.int32, (BLOCK, columns), 1) < HEAD_DIM
    window = 3 * BLOCK
    keys = window + GLOBALS + R * BLOCK
    key_column = lax.broadcasted_iota(jnp.int32, (1, keys), 1)

    def by_head(rows):
        zero = jnp.zeros_like(rows)
        return jnp.concatenate(
            [jnp.where(first_head, rows, zero), jnp.where(first_head, zero, rows)], axis=0
        )

    def joined(pair):
        return jnp.where(first_head, pair[:BLOCK], pair[BLOCK:])

    def dot(a, b, dims):
        return lax.dot_general(a, b, (dims, ((), ())), preferred_element_type=f32)

    room = GLOBALS if arrived.shape[1] % PAIR == 0 else arrived.shape[1] % PAIR // 2
    first_row = arrived.shape[1] - 2 * room
    packed = lax.broadcasted_iota(jnp.int32, (GLOBALS, LANES * room), 1)
    chosen = jnp.where(packed == global_place[...], 1.0, 0.0).astype(bf16)
    for half in range(2):
        begin = first_row + half * room
        rows = [arrived[lane, begin : begin + room, :] for lane in range(LANES)]
        panel[half * GLOBALS : (half + 1) * GLOBALS, :] = dot(
            chosen, jnp.concatenate(rows, axis=0), ((1,), (0,))
        ).astype(bf16)

    def one(block, carry):
        row = pl.multiple_of(block * BLOCK, BLOCK)
        here = pl.ds(row, BLOCK)
        around = pl.ds(row, window)
        named = [block * R + j for j in range(R)]
        places = [
            (names[n] // blocks % LANES, pl.multiple_of(ranks[n] * PAIR, PAIR)) for n in named
        ]
        kk = jnp.concatenate(
            [key_pad[around, :], panel[:GLOBALS, :]] + [arrived[a, pl.ds(b, BLOCK), :] for a, b in places], axis=0
        )
        vv = jnp.concatenate(
            [value_pad[around, :], panel[GLOBALS:, :]] + [arrived[a, pl.ds(b + BLOCK, BLOCK), :] for a, b in places], axis=0
        )
        q2 = by_head(q[here, :])
        g2 = by_head(g[here, :])
        number = first_block + block
        dead = ((key_column < BLOCK) & (number == 0)) | (
            (key_column >= 2 * BLOCK) & (key_column < window) & (number == last_block)
        )
        scores = dot(q2, kk, ((1,), (1,))) * scale
        scores = jnp.where(dead, -jnp.inf, scores)
        top = jnp.max(scores, axis=-1, keepdims=True)
        raised = jnp.exp(scores - top)
        probs = raised * (1.0 / jnp.sum(raised, axis=-1, keepdims=True))
        probs_b = probs.astype(bf16)
        att = joined(dot(probs_b, vv, ((1,), (0,)))).astype(bf16)
        attended[here, :] = att
        att_f = att.astype(f32)
        delta = jnp.sum(
            g2.astype(f32) * jnp.concatenate([att_f, att_f], axis=0), axis=-1, keepdims=True
        )
        slope = (probs * (dot(g2, vv, ((1,), (1,))) - delta)).astype(bf16)
        query_grad[here, :] = (scale * joined(dot(slope, kk, ((1,), (0,))))).astype(bf16)
        dk = scale * dot(slope, q2, ((0,), (0,)))
        dv = dot(probs_b, g2, ((0,), (0,)))
        key_grad[around, :] += dk[:window]
        value_grad[around, :] += dv[:window]
        panel_grad[:GLOBALS, :] += dk[window : window + GLOBALS]
        panel_grad[GLOBALS:, :] += dv[window : window + GLOBALS]
        for j, (a, b) in enumerate(places):
            first = window + GLOBALS + j * BLOCK
            send[a, pl.ds(b, BLOCK), :] = dk[first : first + BLOCK].astype(bf16)
            send[a, pl.ds(b + BLOCK, BLOCK), :] = dv[first : first + BLOCK].astype(bf16)
        return carry

    lax.fori_loop(0, blocks, one, 0, unroll=R)
    for side, rows in enumerate((pl.ds(0, BLOCK), pl.ds(BLOCK + tokens, BLOCK))):
        rims[side, :BLOCK, :] = key_grad[rows, :].astype(bf16)
        rims[side, BLOCK:, :] = value_grad[rows, :].astype(bf16)
    for half in range(2):
        begin = first_row + half * room
        rows = panel_grad[half * GLOBALS : (half + 1) * GLOBALS, :].astype(bf16)
        rows = dot(chosen, rows, ((0,), (0,))).astype(bf16)
        for lane in range(LANES):
            send[lane, begin : begin + room, :] = rows[lane * room : (lane + 1) * room]


def collect_kernel(asked, global_block, global_row, returned, lane_grads, sums, panel):
    room = panel.shape[0] // 2
    most = asked.shape[0] // LANES
    slots = returned.shape[1] // PAIR if room < GLOBALS else most
    f32 = jnp.float32
    sums[...] = jnp.zeros_like(sums)
    for source in range(LANES):
        for rank in range(slots):
            wanted = asked[source * most + rank]

            @pl.when(wanted >= 0)
            def _():
                rows = returned[source, rank * PAIR : (rank + 1) * PAIR, :]
                sums[wanted] += rows.astype(f32)

    total_rows = jnp.zeros(panel.shape, f32)
    for lane in range(LANES):
        total_rows += returned[lane, slots * PAIR :, :].astype(f32)
    panel[...] = total_rows

    def spread(number, carry):
        to = global_block[number]

        @pl.when(to >= 0)
        def _():
            for half in range(2):
                sums[to, pl.ds(global_row[number] + half * BLOCK, 1), :] += panel[
                    pl.ds(number + half * room, 1), :
                ]

        return carry

    lax.fori_loop(0, room, spread, 0)
    lane_grads[...] = sums[...].astype(lane_grads.dtype)


def finish_kernel(
    key_grad,
    value_grad,
    from_left,
    from_right,
    others,
    key_out,
    value_out,
    key_sum,
    value_sum,
):
    tokens = key_out.shape[0]
    f32 = jnp.float32

    def own(block, carry):
        row = pl.multiple_of(block * BLOCK, BLOCK)
        here, padded = pl.ds(row, BLOCK), pl.ds(row + BLOCK, BLOCK)
        key_sum[here, :] = key_grad[padded, :] + others[block, :BLOCK, :].astype(f32)
        value_sum[here, :] = value_grad[padded, :] + others[block, BLOCK:, :].astype(f32)
        return carry

    lax.fori_loop(0, others.shape[0], own, 0)
    key_sum[:BLOCK, :] += from_left[:BLOCK, :].astype(f32)
    value_sum[:BLOCK, :] += from_left[BLOCK:, :].astype(f32)
    key_sum[tokens - BLOCK :, :] += from_right[:BLOCK, :].astype(f32)
    value_sum[tokens - BLOCK :, :] += from_right[BLOCK:, :].astype(f32)

    key_out[...] = key_sum[...].astype(key_out.dtype)
    value_out[...] = value_sum[...].astype(value_out.dtype)


def exchange(array, axis):
    return lax.all_to_all(array, axis, split_axis=0, concat_axis=0, tiled=True)


def spread(array, axis):
    return exchange(jnp.broadcast_to(array, (lax.axis_size(axis),) + array.shape), axis)


def shards(queries, key_states, value_states, out_weight, output_grad, rand_blocks, global_pos):
    bf16, f32 = jnp.bfloat16, jnp.float32
    tokens, columns = queries.shape
    blocks = tokens // BLOCK
    slabs, heads = lax.axis_size("slab"), lax.axis_size("head")
    slab, me, head = lax.axis_index("slab"), lax.axis_index("lane"), lax.axis_index("head")
    position, seq_count = slab * LANES + me, slabs * LANES
    smem, vmem = whole(pltpu.SMEM), whole()

    own = jnp.concatenate(
        [key_states.reshape(blocks, BLOCK, columns), value_states.reshape(blocks, BLOCK, columns)],
        axis=1,
    )
    lane_blocks = lax.all_gather(own, "slab", axis=0, tiled=True)

    names = rand_blocks.reshape(-1)
    owner = names // blocks
    lane, code = owner % LANES, owner // LANES * blocks + names % blocks
    number = jnp.arange(names.shape[0])
    same = (lane[:, None] == lane[None, :]) & (number[None, :] < number[:, None])
    ranks = jnp.sum(same.astype(jnp.int32), axis=1)
    index = jnp.arange(LANES * slabs)
    hit = (lane * slabs + ranks)[None, :] == index[:, None]
    wanted = jnp.max(jnp.where(hit, code[None, :], -1), axis=1).reshape(LANES, slabs)
    load = jnp.broadcast_to(jnp.max(ranks) + 1, (LANES, 1))
    global_lane = global_pos // tokens % LANES
    number = jnp.arange(GLOBALS)
    same = (global_lane[:, None] == global_lane[None, :]) & (number[None, :] < number[:, None])
    global_rank = jnp.sum(same.astype(jnp.int32), axis=1)
    hit = (global_rank[None, :] == number[:, None]) & (global_lane == me)[None, :]
    global_block = global_pos // tokens // LANES * blocks + global_pos % tokens // BLOCK
    global_block = jnp.max(jnp.where(hit, global_block[None, :], -1), axis=1)
    global_row = jnp.max(jnp.where(hit, (global_pos % BLOCK)[None, :], 0), axis=1)
    heard = exchange(jnp.concatenate([wanted, load], axis=1), "lane")
    asked = heard[:, :slabs].reshape(-1)
    load = jnp.max(spread(jnp.max(heard[:, slabs:]).reshape(1), "slab"))
    fits = (load <= FEW) & (jnp.max(global_rank) < FEW_ROWS)

    partial_grad = lax.dot_general(
        output_grad, out_weight, (((1,), (1,)), ((), ())), preferred_element_type=f32
    )
    partial_grad = partial_grad.reshape(tokens, heads, columns).transpose(1, 0, 2)
    grad_att = jnp.sum(exchange(partial_grad, "head"), axis=0).astype(bf16)

    seq = ("slab", "lane")
    forth = [(i, i + 1) for i in range(seq_count - 1)]
    back = [(i + 1, i) for i in range(seq_count - 1)]
    left = lax.ppermute(own[blocks - 1], seq, forth)
    right = lax.ppermute(own[0], seq, back)

    order = (head - jnp.arange(heads)) % heads
    weight_rows = out_weight.reshape(heads, columns, -1).at[order].get(mode="promise_in_bounds")
    weight_rows = weight_rows.reshape(out_weight.shape)
    beside = (lane_blocks, asked, fits, grad_att, left, right, weight_rows)
    beside = lax.optimization_barrier(beside + (global_lane, global_rank, global_block, global_row))
    lane_blocks, asked, fits, grad_att, left, right, weight_rows = beside[:7]
    global_lane, global_rank, global_block, global_row = beside[7:]
    place = jnp.stack([position * blocks, seq_count * blocks - 1]).astype(jnp.int32)
    padded = tokens + PAIR

    def middle(slots, room):
        sent_rows = slots * PAIR + 2 * room
        global_place = (global_lane * room + global_rank).reshape(GLOBALS, 1)
        served = call(
            serve_kernel,
            shape((LANES, sent_rows, columns), bf16),
            [smem, smem, smem, vmem],
            [pltpu.VMEM((2 * room, columns), f32)],
            moved=8 << 20,
        )(asked, global_block, global_row, lane_blocks)
        arrived = exchange(served, "lane")
        attended, query_grad, key_part, value_part, rims, sent = call(
            attention_kernel,
            (
                shape((tokens, columns), bf16),
                shape((tokens, columns), bf16),
                shape((padded, columns), f32),
                shape((padded, columns), f32),
                shape((2, PAIR, columns), bf16),
                shape((LANES, sent_rows, columns), bf16),
            ),
            [smem, smem, smem] + [vmem] * 8,
            [pltpu.VMEM((padded, columns), bf16)] * 2
            + [
                pltpu.VMEM((2 * GLOBALS, columns), bf16),
                pltpu.VMEM((2 * GLOBALS, columns), f32),
            ],
            flops=1 << 30,
            moved=12 << 20,
        )(
            place,
            names,
            ranks,
            queries,
            grad_att,
            key_states,
            value_states,
            left,
            right,
            global_place,
            arrived,
        )
        returned = exchange(sent, "lane")

        pieces = [attended] + [
            lax.ppermute(attended, "head", [(i, (i + k) % heads) for i in range(heads)])
            for k in range(1, heads)
        ]
        from_left = lax.ppermute(rims[1], seq, forth)
        from_right = lax.ppermute(rims[0], seq, back)
        everywhere = jnp.concatenate(pieces, axis=1)
        weight_part = lax.dot_general(
            everywhere, output_grad, (((0,), (0,)), ((), ())), preferred_element_type=f32
        ) * (1.0 / math.sqrt(tokens * seq_count))
        returned, from_left, from_right, weight_part = lax.optimization_barrier(
            (returned, from_left, from_right, weight_part)
        )
        lane_grads = call(
            collect_kernel,
            shape((slabs * blocks, PAIR, columns), bf16),
            [smem, smem, smem, vmem],
            [
                pltpu.VMEM((slabs * blocks, PAIR, columns), f32),
                pltpu.VMEM((2 * room, columns), f32),
            ],
            moved=10 << 20,
        )(asked, global_block, global_row, returned)
        return (
            everywhere,
            query_grad,
            key_part,
            value_part,
            from_left,
            from_right,
            weight_part,
            lane_grads,
        )

    few = lambda: middle(FEW, FEW_ROWS)
    all_slots = lambda: middle(slabs, GLOBALS)
    everywhere, query_grad, key_part, value_part, from_left, from_right, weight_part, lane_grads = (
        lax.cond(fits, few, all_slots) if FEW < slabs else all_slots()
    )
    others = lax.psum_scatter(lane_grads, "slab", scatter_dimension=0, tiled=True)

    weight_part = weight_part.reshape(LANES, -1, weight_part.shape[1])
    step = LANES // 2
    while step:
        pair = weight_part.reshape((2, step) + weight_part.shape[1:])
        mine = me // step % 2
        kept = lax.dynamic_index_in_dim(pair, mine, 0, keepdims=False)
        other = lax.dynamic_index_in_dim(pair, 1 - mine, 0, keepdims=False)
        other = lax.ppermute(other, "lane", [(i, i ^ step) for i in range(LANES)])
        weight_part = kept + other
        step //= 2
    features = weight_part.shape[-1]
    share = jnp.sum(exchange(weight_part.reshape(slabs, -1, features), "slab"), axis=0)
    share = spread(share, "slab").reshape(-1, features)
    weight_grad = spread(share, "lane").reshape(heads, columns, features)
    weight_grad = weight_grad.at[order].get(mode="promise_in_bounds")
    weight_grad = weight_grad.reshape(heads * columns, features)

    projected = jnp.dot(everywhere, weight_rows, preferred_element_type=f32).astype(bf16)
    key_grad, value_grad = call(
        finish_kernel,
        (shape((tokens, columns), bf16), shape((tokens, columns), bf16)),
        [vmem] * 5,
        [pltpu.VMEM((tokens, columns), f32)] * 2,
        moved=2 << 20,
    )(key_part, value_part, from_left, from_right, others)
    return projected, query_grad, key_grad, value_grad, weight_grad


def solution(mesh):
    seq_count, head_count = mesh.devices.shape
    fine = Mesh(
        mesh.devices.reshape(seq_count // LANES, LANES, head_count), ("slab", "lane", "head")
    )
    seq = ("slab", "lane")
    placed = (
        P(seq, "head"),
        P(seq, "head"),
        P(seq, "head"),
        P(None, "head"),
        P(seq, "head"),
        P(seq, None),
        P(),
    )
    return jax.shard_map(
        shards,
        mesh=fine,
        in_specs=placed,
        out_specs=(
            P(seq, "head"),
            P(seq, "head"),
            P(seq, "head"),
            P(seq, "head"),
            P(None, "head"),
        ),
        check_vma=False,
    )
```

```python
import functools
import math

import jax
import jax.numpy as jnp
from jax import lax
from jax.experimental import pallas as pl
from jax.experimental.pallas import tpu as pltpu
from jax.sharding import Mesh
from jax.sharding import PartitionSpec as P

HEAD_DIM = 64
BLOCK = 64
PAIR = 2 * BLOCK
LANES = 8
TILE = 16
FEW = (8, 9, 10)
FEW_ROWS = 32
R = 3
GLOBALS = 128
VMEM_LIMIT = 40 * 1024 * 1024


def whole(space=pltpu.VMEM):
    return pl.BlockSpec(memory_space=space)


def shape(dims, dtype):
    return jax.ShapeDtypeStruct(dims, dtype)


def call(kernel, out_shape, in_specs, scratch=(), flops=0, moved=0):
    return pl.pallas_call(
        kernel,
        out_shape=out_shape,
        in_specs=in_specs,
        out_specs=jax.tree.map(lambda _: whole(), out_shape),
        scratch_shapes=list(scratch),
        compiler_params=pltpu.CompilerParams(vmem_limit_bytes=VMEM_LIMIT),
        cost_estimate=pl.CostEstimate(flops=flops, bytes_accessed=moved, transcendentals=0),
    )


def serve_kernel(asked, global_block, global_row, lane_blocks, send, panel):
    room = panel.shape[0] // 2
    most = asked.shape[0] // LANES
    slots = send.shape[1] // PAIR if room < GLOBALS else most
    for to in range(LANES):
        for rank in range(slots):
            wanted = jnp.maximum(asked[to * most + rank], 0)
            send[to, rank * PAIR : (rank + 1) * PAIR, :] = lane_blocks[wanted]

    panel[...] = jnp.zeros_like(panel)
    row_number = lax.broadcasted_iota(jnp.int32, (TILE, panel.shape[1]), 0)

    def pick(number, carry):
        source, inside = global_block[number], global_row[number]

        @pl.when(source >= 0)
        def _():
            first = pl.multiple_of(inside // TILE * TILE, TILE)
            hit = row_number == inside % TILE
            for half in range(2):
                rows = lane_blocks[source, pl.ds(first + half * BLOCK, TILE), :]
                panel[pl.ds(number + half * room, 1), :] = jnp.sum(
                    jnp.where(hit, rows.astype(jnp.float32), 0.0), axis=0, keepdims=True
                )

        return carry

    lax.fori_loop(0, room, pick, 0)
    panel_rows = panel[...].astype(send.dtype)
    for to in range(LANES):
        send[to, slots * PAIR :, :] = panel_rows


def attention_kernel(
    place,
    names,
    ranks,
    q,
    g,
    key,
    value,
    left,
    right,
    global_place,
    arrived,
    attended,
    query_grad,
    key_grad,
    value_grad,
    rims,
    send,
    key_pad,
    value_pad,
    panel,
    panel_grad,
):
    tokens, columns = q.shape
    blocks = tokens // BLOCK
    scale = 1.0 / math.sqrt(HEAD_DIM)
    f32, bf16 = jnp.float32, jnp.bfloat16
    key_pad[:BLOCK, :] = left[:BLOCK, :]
    value_pad[:BLOCK, :] = left[BLOCK:, :]
    key_pad[BLOCK : BLOCK + tokens, :] = key[...]
    value_pad[BLOCK : BLOCK + tokens, :] = value[...]
    key_pad[BLOCK + tokens :, :] = right[:BLOCK, :]
    value_pad[BLOCK + tokens :, :] = right[BLOCK:, :]
    key_grad[...] = jnp.zeros_like(key_grad)
    value_grad[...] = jnp.zeros_like(value_grad)
    panel_grad[...] = jnp.zeros_like(panel_grad)
    first_block, last_block = place[0], place[1]
    first_head = lax.broadcasted_iota(jnp.int32, (BLOCK, columns), 1) < HEAD_DIM
    window = 3 * BLOCK
    keys = window + GLOBALS + R * BLOCK
    key_column = lax.broadcasted_iota(jnp.int32, (1, keys), 1)

    def by_head(rows):
        zero = jnp.zeros_like(rows)
        return jnp.concatenate(
            [jnp.where(first_head, rows, zero), jnp.where(first_head, zero, rows)], axis=0
        )

    def joined(pair):
        return jnp.where(first_head, pair[:BLOCK], pair[BLOCK:])

    def dot(a, b, dims):
        return lax.dot_general(a, b, (dims, ((), ())), preferred_element_type=f32)

    room = GLOBALS if arrived.shape[1] % PAIR == 0 else arrived.shape[1] % PAIR // 2
    first_row = arrived.shape[1] - 2 * room
    packed = lax.broadcasted_iota(jnp.int32, (GLOBALS, LANES * room), 1)
    chosen = jnp.where(packed == global_place[...], 1.0, 0.0).astype(bf16)
    for half in range(2):
        begin = first_row + half * room
        rows = [arrived[lane, begin : begin + room, :] for lane in range(LANES)]
        panel[half * GLOBALS : (half + 1) * GLOBALS, :] = dot(
            chosen, jnp.concatenate(rows, axis=0), ((1,), (0,))
        ).astype(bf16)

    def one(block, carry):
        row = pl.multiple_of(block * BLOCK, BLOCK)
        here = pl.ds(row, BLOCK)
        around = pl.ds(row, window)
        named = [block * R + j for j in range(R)]
        places = [
            (names[n] // blocks % LANES, pl.multiple_of(ranks[n] * PAIR, PAIR)) for n in named
        ]
        kk = jnp.concatenate(
            [key_pad[around, :], panel[:GLOBALS, :]] + [arrived[a, pl.ds(b, BLOCK), :] for a, b in places], axis=0
        )
        vv = jnp.concatenate(
            [value_pad[around, :], panel[GLOBALS:, :]] + [arrived[a, pl.ds(b + BLOCK, BLOCK), :] for a, b in places], axis=0
        )
        q2 = by_head(q[here, :])
        g2 = by_head(g[here, :])
        number = first_block + block
        dead = ((key_column < BLOCK) & (number == 0)) | (
            (key_column >= 2 * BLOCK) & (key_column < window) & (number == last_block)
        )
        scores = dot(q2, kk, ((1,), (1,))) * scale
        scores = jnp.where(dead, -jnp.inf, scores)
        top = jnp.max(scores, axis=-1, keepdims=True)
        raised = jnp.exp(scores - top)
        probs = raised * (1.0 / jnp.sum(raised, axis=-1, keepdims=True))
        probs_b = probs.astype(bf16)
        att = joined(dot(probs_b, vv, ((1,), (0,)))).astype(bf16)
        attended[here, :] = att
        att_f = att.astype(f32)
        delta = jnp.sum(
            g2.astype(f32) * jnp.concatenate([att_f, att_f], axis=0), axis=-1, keepdims=True
        )
        slope = (probs * (dot(g2, vv, ((1,), (1,))) - delta)).astype(bf16)
        query_grad[here, :] = (scale * joined(dot(slope, kk, ((1,), (0,))))).astype(bf16)
        dk = scale * dot(slope, q2, ((0,), (0,)))
        dv = dot(probs_b, g2, ((0,), (0,)))
        key_grad[around, :] += dk[:window]
        value_grad[around, :] += dv[:window]
        panel_grad[:GLOBALS, :] += dk[window : window + GLOBALS]
        panel_grad[GLOBALS:, :] += dv[window : window + GLOBALS]
        for j, (a, b) in enumerate(places):
            first = window + GLOBALS + j * BLOCK
            send[a, pl.ds(b, BLOCK), :] = dk[first : first + BLOCK].astype(bf16)
            send[a, pl.ds(b + BLOCK, BLOCK), :] = dv[first : first + BLOCK].astype(bf16)
        return carry

    lax.fori_loop(0, blocks, one, 0, unroll=R)
    for side, rows in enumerate((pl.ds(0, BLOCK), pl.ds(BLOCK + tokens, BLOCK))):
        rims[side, :BLOCK, :] = key_grad[rows, :].astype(bf16)
        rims[side, BLOCK:, :] = value_grad[rows, :].astype(bf16)
    for half in range(2):
        begin = first_row + half * room
        rows = panel_grad[half * GLOBALS : (half + 1) * GLOBALS, :].astype(bf16)
        rows = dot(chosen, rows, ((0,), (0,))).astype(bf16)
        for lane in range(LANES):
            send[lane, begin : begin + room, :] = rows[lane * room : (lane + 1) * room]


def collect_kernel(asked, global_block, global_row, returned, lane_grads, sums, panel):
    room = panel.shape[0] // 2
    most = asked.shape[0] // LANES
    slots = returned.shape[1] // PAIR if room < GLOBALS else most
    f32 = jnp.float32
    sums[...] = jnp.zeros_like(sums)
    for source in range(LANES):
        for rank in range(slots):
            wanted = asked[source * most + rank]

            @pl.when(wanted >= 0)
            def _():
                rows = returned[source, rank * PAIR : (rank + 1) * PAIR, :]
                sums[wanted] += rows.astype(f32)

    total_rows = jnp.zeros(panel.shape, f32)
    for lane in range(LANES):
        total_rows += returned[lane, slots * PAIR :, :].astype(f32)
    panel[...] = total_rows

    def spread(number, carry):
        to = global_block[number]

        @pl.when(to >= 0)
        def _():
            for half in range(2):
                sums[to, pl.ds(global_row[number] + half * BLOCK, 1), :] += panel[
                    pl.ds(number + half * room, 1), :
                ]

        return carry

    lax.fori_loop(0, room, spread, 0)
    lane_grads[...] = sums[...].astype(lane_grads.dtype)


def finish_kernel(
    key_grad,
    value_grad,
    from_left,
    from_right,
    others,
    key_out,
    value_out,
    key_sum,
    value_sum,
):
    tokens = key_out.shape[0]
    f32 = jnp.float32

    def own(block, carry):
        row = pl.multiple_of(block * BLOCK, BLOCK)
        here, padded = pl.ds(row, BLOCK), pl.ds(row + BLOCK, BLOCK)
        key_sum[here, :] = key_grad[padded, :] + others[block, :BLOCK, :].astype(f32)
        value_sum[here, :] = value_grad[padded, :] + others[block, BLOCK:, :].astype(f32)
        return carry

    lax.fori_loop(0, others.shape[0], own, 0)
    key_sum[:BLOCK, :] += from_left[:BLOCK, :].astype(f32)
    value_sum[:BLOCK, :] += from_left[BLOCK:, :].astype(f32)
    key_sum[tokens - BLOCK :, :] += from_right[:BLOCK, :].astype(f32)
    value_sum[tokens - BLOCK :, :] += from_right[BLOCK:, :].astype(f32)

    key_out[...] = key_sum[...].astype(key_out.dtype)
    value_out[...] = value_sum[...].astype(value_out.dtype)


def exchange(array, axis):
    return lax.all_to_all(array, axis, split_axis=0, concat_axis=0, tiled=True)


def spread(array, axis):
    return exchange(jnp.broadcast_to(array, (lax.axis_size(axis),) + array.shape), axis)


def shards(queries, key_states, value_states, out_weight, output_grad, rand_blocks, global_pos):
    bf16, f32 = jnp.bfloat16, jnp.float32
    tokens, columns = queries.shape
    blocks = tokens // BLOCK
    slabs, heads = lax.axis_size("slab"), lax.axis_size("head")
    slab, me, head = lax.axis_index("slab"), lax.axis_index("lane"), lax.axis_index("head")
    position, seq_count = slab * LANES + me, slabs * LANES
    smem, vmem = whole(pltpu.SMEM), whole()

    own = jnp.concatenate(
        [key_states.reshape(blocks, BLOCK, columns), value_states.reshape(blocks, BLOCK, columns)],
        axis=1,
    )
    lane_blocks = lax.all_gather(own, "slab", axis=0, tiled=True)

    names = rand_blocks.reshape(-1)
    owner = names // blocks
    lane, code = owner % LANES, owner // LANES * blocks + names % blocks
    number = jnp.arange(names.shape[0])
    same = (lane[:, None] == lane[None, :]) & (number[None, :] < number[:, None])
    ranks = jnp.sum(same.astype(jnp.int32), axis=1)
    index = jnp.arange(LANES * slabs)
    hit = (lane * slabs + ranks)[None, :] == index[:, None]
    wanted = jnp.max(jnp.where(hit, code[None, :], -1), axis=1).reshape(LANES, slabs)
    load = jnp.broadcast_to(jnp.max(ranks) + 1, (LANES, 1))
    global_lane = global_pos // tokens % LANES
    number = jnp.arange(GLOBALS)
    same = (global_lane[:, None] == global_lane[None, :]) & (number[None, :] < number[:, None])
    global_rank = jnp.sum(same.astype(jnp.int32), axis=1)
    hit = (global_rank[None, :] == number[:, None]) & (global_lane == me)[None, :]
    global_block = global_pos // tokens // LANES * blocks + global_pos % tokens // BLOCK
    global_block = jnp.max(jnp.where(hit, global_block[None, :], -1), axis=1)
    global_row = jnp.max(jnp.where(hit, (global_pos % BLOCK)[None, :], 0), axis=1)
    heard = exchange(jnp.concatenate([wanted, load], axis=1), "lane")
    asked = heard[:, :slabs].reshape(-1)
    load = jnp.max(spread(jnp.max(heard[:, slabs:]).reshape(1), "slab"))
    choice = jnp.sum((load > jnp.array(FEW)).astype(jnp.int32))
    choice = jnp.where(jnp.max(global_rank) < FEW_ROWS, choice, len(FEW))

    partial_grad = lax.dot_general(
        output_grad, out_weight, (((1,), (1,)), ((), ())), preferred_element_type=f32
    )
    partial_grad = partial_grad.reshape(tokens, heads, columns).transpose(1, 0, 2)
    grad_att = jnp.sum(exchange(partial_grad, "head"), axis=0).astype(bf16)

    seq = ("slab", "lane")
    forth = [(i, i + 1) for i in range(seq_count - 1)]
    back = [(i + 1, i) for i in range(seq_count - 1)]
    left = lax.ppermute(own[blocks - 1], seq, forth)
    right = lax.ppermute(own[0], seq, back)

    order = (head - jnp.arange(heads)) % heads
    weight_rows = out_weight.reshape(heads, columns, -1).at[order].get(mode="promise_in_bounds")
    weight_rows = weight_rows.reshape(out_weight.shape)
    beside = (lane_blocks, asked, choice, grad_att, left, right, weight_rows)
    beside = lax.optimization_barrier(beside + (global_lane, global_rank, global_block, global_row))
    lane_blocks, asked, choice, grad_att, left, right, weight_rows = beside[:7]
    global_lane, global_rank, global_block, global_row = beside[7:]
    place = jnp.stack([position * blocks, seq_count * blocks - 1]).astype(jnp.int32)
    padded = tokens + PAIR

    def middle(slots, room):
        sent_rows = slots * PAIR + 2 * room
        global_place = (global_lane * room + global_rank).reshape(GLOBALS, 1)
        served = call(
            serve_kernel,
            shape((LANES, sent_rows, columns), bf16),
            [smem, smem, smem, vmem],
            [pltpu.VMEM((2 * room, columns), f32)],
            moved=8 << 20,
        )(asked, global_block, global_row, lane_blocks)
        arrived = exchange(served, "lane")
        attended, query_grad, key_part, value_part, rims, sent = call(
            attention_kernel,
            (
                shape((tokens, columns), bf16),
                shape((tokens, columns), bf16),
                shape((padded, columns), f32),
                shape((padded, columns), f32),
                shape((2, PAIR, columns), bf16),
                shape((LANES, sent_rows, columns), bf16),
            ),
            [smem, smem, smem] + [vmem] * 8,
            [pltpu.VMEM((padded, columns), bf16)] * 2
            + [
                pltpu.VMEM((2 * GLOBALS, columns), bf16),
                pltpu.VMEM((2 * GLOBALS, columns), f32),
            ],
            flops=1 << 30,
            moved=12 << 20,
        )(
            place,
            names,
            ranks,
            queries,
            grad_att,
            key_states,
            value_states,
            left,
            right,
            global_place,
            arrived,
        )
        returned = exchange(sent, "lane")

        pieces = [attended] + [
            lax.ppermute(attended, "head", [(i, (i + k) % heads) for i in range(heads)])
            for k in range(1, heads)
        ]
        from_left = lax.ppermute(rims[1], seq, forth)
        from_right = lax.ppermute(rims[0], seq, back)
        everywhere = jnp.concatenate(pieces, axis=1)
        weight_part = lax.dot_general(
            everywhere, output_grad, (((0,), (0,)), ((), ())), preferred_element_type=f32
        ) * (1.0 / math.sqrt(tokens * seq_count))
        returned, from_left, from_right, weight_part = lax.optimization_barrier(
            (returned, from_left, from_right, weight_part)
        )
        lane_grads = call(
            collect_kernel,
            shape((slabs * blocks, PAIR, columns), bf16),
            [smem, smem, smem, vmem],
            [
                pltpu.VMEM((slabs * blocks, PAIR, columns), f32),
                pltpu.VMEM((2 * room, columns), f32),
            ],
            moved=10 << 20,
        )(asked, global_block, global_row, returned)
        return (
            everywhere,
            query_grad,
            key_part,
            value_part,
            from_left,
            from_right,
            weight_part,
            lane_grads,
        )

    branches = [functools.partial(middle, slots, FEW_ROWS) for slots in FEW]
    branches.append(functools.partial(middle, slabs, GLOBALS))
    everywhere, query_grad, key_part, value_part, from_left, from_right, weight_part, lane_grads = (
        lax.switch(choice, branches)
    )
    others = lax.psum_scatter(lane_grads, "slab", scatter_dimension=0, tiled=True)

    weight_part = weight_part.reshape(LANES, -1, weight_part.shape[1])
    step = LANES // 2
    while step:
        pair = weight_part.reshape((2, step) + weight_part.shape[1:])
        mine = me // step % 2
        kept = lax.dynamic_index_in_dim(pair, mine, 0, keepdims=False)
        other = lax.dynamic_index_in_dim(pair, 1 - mine, 0, keepdims=False)
        other = lax.ppermute(other, "lane", [(i, i ^ step) for i in range(LANES)])
        weight_part = kept + other
        step //= 2
    features = weight_part.shape[-1]
    share = jnp.sum(exchange(weight_part.reshape(slabs, -1, features), "slab"), axis=0)
    share = spread(share, "slab").reshape(-1, features)
    weight_grad = spread(share, "lane").reshape(heads, columns, features)
    weight_grad = weight_grad.at[order].get(mode="promise_in_bounds")
    weight_grad = weight_grad.reshape(heads * columns, features)

    projected = jnp.dot(everywhere, weight_rows, preferred_element_type=f32).astype(bf16)
    key_grad, value_grad = call(
        finish_kernel,
        (shape((tokens, columns), bf16), shape((tokens, columns), bf16)),
        [vmem] * 5,
        [pltpu.VMEM((tokens, columns), f32)] * 2,
        moved=2 << 20,
    )(key_part, value_part, from_left, from_right, others)
    return projected, query_grad, key_grad, value_grad, weight_grad


def solution(mesh):
    seq_count, head_count = mesh.devices.shape
    fine = Mesh(
        mesh.devices.reshape(seq_count // LANES, LANES, head_count), ("slab", "lane", "head")
    )
    seq = ("slab", "lane")
    placed = (
        P(seq, "head"),
        P(seq, "head"),
        P(seq, "head"),
        P(None, "head"),
        P(seq, "head"),
        P(seq, None),
        P(),
    )
    return jax.shard_map(
        shards,
        mesh=fine,
        in_specs=placed,
        out_specs=(
            P(seq, "head"),
            P(seq, "head"),
            P(seq, "head"),
            P(seq, "head"),
            P(None, "head"),
        ),
        check_vma=False,
    )
```

```python
import functools
import math

import jax
import jax.numpy as jnp
from jax import lax
from jax.experimental import pallas as pl
from jax.experimental.pallas import tpu as pltpu
from jax.sharding import Mesh
from jax.sharding import PartitionSpec as P

HEAD_DIM = 64
BLOCK = 64
PAIR = 2 * BLOCK
LANES = 8
TILE = 16
FEW = (8, 9, 10)
FEW_ROWS = 32
R = 3
GLOBALS = 128
VMEM_LIMIT = 40 * 1024 * 1024


def whole(space=pltpu.VMEM):
    return pl.BlockSpec(memory_space=space)


def shape(dims, dtype):
    return jax.ShapeDtypeStruct(dims, dtype)


def call(kernel, out_shape, in_specs, scratch=(), flops=0, moved=0):
    return pl.pallas_call(
        kernel,
        out_shape=out_shape,
        in_specs=in_specs,
        out_specs=jax.tree.map(lambda _: whole(), out_shape),
        scratch_shapes=list(scratch),
        compiler_params=pltpu.CompilerParams(vmem_limit_bytes=VMEM_LIMIT),
        cost_estimate=pl.CostEstimate(flops=flops, bytes_accessed=moved, transcendentals=0),
    )


def serve_kernel(asked, global_block, global_row, lane_blocks, send, panel):
    room = panel.shape[0] // 2
    most = asked.shape[0] // LANES
    slots = send.shape[1] // PAIR if room < GLOBALS else most
    for to in range(LANES):
        for rank in range(slots):
            wanted = jnp.maximum(asked[to * most + rank], 0)
            send[to, rank * PAIR : (rank + 1) * PAIR, :] = lane_blocks[wanted]

    panel[...] = jnp.zeros_like(panel)
    row_number = lax.broadcasted_iota(jnp.int32, (TILE, panel.shape[1]), 0)

    def pick(number, carry):
        source, inside = global_block[number], global_row[number]

        @pl.when(source >= 0)
        def _():
            first = pl.multiple_of(inside // TILE * TILE, TILE)
            hit = row_number == inside % TILE
            for half in range(2):
                rows = lane_blocks[source, pl.ds(first + half * BLOCK, TILE), :]
                panel[pl.ds(number + half * room, 1), :] = jnp.sum(
                    jnp.where(hit, rows.astype(jnp.float32), 0.0), axis=0, keepdims=True
                )

        return carry

    lax.fori_loop(0, room, pick, 0)
    panel_rows = panel[...].astype(send.dtype)
    for to in range(LANES):
        send[to, slots * PAIR :, :] = panel_rows


def attention_kernel(
    place,
    names,
    ranks,
    q,
    g,
    key,
    value,
    left,
    right,
    global_place,
    arrived,
    attended,
    query_grad,
    key_grad,
    value_grad,
    rims,
    send,
    key_pad,
    value_pad,
    panel,
    panel_grad,
):
    tokens, columns = q.shape
    blocks = tokens // BLOCK
    scale = 1.0 / math.sqrt(HEAD_DIM)
    f32, bf16 = jnp.float32, jnp.bfloat16
    key_pad[:BLOCK, :] = left[:BLOCK, :]
    value_pad[:BLOCK, :] = left[BLOCK:, :]
    key_pad[BLOCK : BLOCK + tokens, :] = key[...]
    value_pad[BLOCK : BLOCK + tokens, :] = value[...]
    key_pad[BLOCK + tokens :, :] = right[:BLOCK, :]
    value_pad[BLOCK + tokens :, :] = right[BLOCK:, :]
    key_grad[...] = jnp.zeros_like(key_grad)
    value_grad[...] = jnp.zeros_like(value_grad)
    panel_grad[...] = jnp.zeros_like(panel_grad)
    first_block, last_block = place[0], place[1]
    first_head = lax.broadcasted_iota(jnp.int32, (BLOCK, columns), 1) < HEAD_DIM
    window = 3 * BLOCK
    keys = window + GLOBALS + R * BLOCK
    key_column = lax.broadcasted_iota(jnp.int32, (1, keys), 1)

    def by_head(rows):
        zero = jnp.zeros_like(rows)
        return jnp.concatenate(
            [jnp.where(first_head, rows, zero), jnp.where(first_head, zero, rows)], axis=0
        )

    def joined(pair):
        return jnp.where(first_head, pair[:BLOCK], pair[BLOCK:])

    def dot(a, b, dims):
        return lax.dot_general(a, b, (dims, ((), ())), preferred_element_type=f32)

    room = GLOBALS if arrived.shape[1] % PAIR == 0 else arrived.shape[1] % PAIR // 2
    first_row = arrived.shape[1] - 2 * room
    packed = lax.broadcasted_iota(jnp.int32, (GLOBALS, LANES * room), 1)
    chosen = jnp.where(packed == global_place[...], 1.0, 0.0).astype(bf16)
    for half in range(2):
        begin = first_row + half * room
        rows = [arrived[lane, begin : begin + room, :] for lane in range(LANES)]
        panel[half * GLOBALS : (half + 1) * GLOBALS, :] = dot(
            chosen, jnp.concatenate(rows, axis=0), ((1,), (0,))
        ).astype(bf16)

    def one(block, carry):
        row = pl.multiple_of(block * BLOCK, BLOCK)
        here = pl.ds(row, BLOCK)
        around = pl.ds(row, window)
        named = [block * R + j for j in range(R)]
        places = [
            (names[n] // blocks % LANES, pl.multiple_of(ranks[n] * PAIR, PAIR)) for n in named
        ]
        kk = jnp.concatenate(
            [key_pad[around, :], panel[:GLOBALS, :]] + [arrived[a, pl.ds(b, BLOCK), :] for a, b in places], axis=0
        )
        vv = jnp.concatenate(
            [value_pad[around, :], panel[GLOBALS:, :]] + [arrived[a, pl.ds(b + BLOCK, BLOCK), :] for a, b in places], axis=0
        )
        q2 = by_head(q[here, :])
        g2 = by_head(g[here, :])
        number = first_block + block
        dead = ((key_column < BLOCK) & (number == 0)) | (
            (key_column >= 2 * BLOCK) & (key_column < window) & (number == last_block)
        )
        scores = dot(q2, kk, ((1,), (1,))) * scale
        scores = jnp.where(dead, -jnp.inf, scores)
        top = jnp.max(scores, axis=-1, keepdims=True)
        raised = jnp.exp(scores - top)
        probs = raised * (1.0 / jnp.sum(raised, axis=-1, keepdims=True))
        probs_b = probs.astype(bf16)
        att = joined(dot(probs_b, vv, ((1,), (0,)))).astype(bf16)
        attended[here, :] = att
        att_f = att.astype(f32)
        delta = jnp.sum(
            g2.astype(f32) * jnp.concatenate([att_f, att_f], axis=0), axis=-1, keepdims=True
        )
        slope = (probs * (dot(g2, vv, ((1,), (1,))) - delta)).astype(bf16)
        query_grad[here, :] = (scale * joined(dot(slope, kk, ((1,), (0,))))).astype(bf16)
        dk = scale * dot(slope, q2, ((0,), (0,)))
        dv = dot(probs_b, g2, ((0,), (0,)))
        key_grad[around, :] += dk[:window]
        value_grad[around, :] += dv[:window]
        panel_grad[:GLOBALS, :] += dk[window : window + GLOBALS]
        panel_grad[GLOBALS:, :] += dv[window : window + GLOBALS]
        for j, (a, b) in enumerate(places):
            first = window + GLOBALS + j * BLOCK
            send[a, pl.ds(b, BLOCK), :] = dk[first : first + BLOCK].astype(bf16)
            send[a, pl.ds(b + BLOCK, BLOCK), :] = dv[first : first + BLOCK].astype(bf16)
        return carry

    lax.fori_loop(0, blocks, one, 0, unroll=True)
    for side, rows in enumerate((pl.ds(0, BLOCK), pl.ds(BLOCK + tokens, BLOCK))):
        rims[side, :BLOCK, :] = key_grad[rows, :].astype(bf16)
        rims[side, BLOCK:, :] = value_grad[rows, :].astype(bf16)
    for half in range(2):
        begin = first_row + half * room
        rows = panel_grad[half * GLOBALS : (half + 1) * GLOBALS, :].astype(bf16)
        rows = dot(chosen, rows, ((0,), (0,))).astype(bf16)
        for lane in range(LANES):
            send[lane, begin : begin + room, :] = rows[lane * room : (lane + 1) * room]


def collect_kernel(asked, global_block, global_row, returned, lane_grads, sums, panel):
    room = panel.shape[0] // 2
    most = asked.shape[0] // LANES
    slots = returned.shape[1] // PAIR if room < GLOBALS else most
    f32 = jnp.float32
    sums[...] = jnp.zeros_like(sums)
    for source in range(LANES):
        for rank in range(slots):
            wanted = asked[source * most + rank]

            @pl.when(wanted >= 0)
            def _():
                rows = returned[source, rank * PAIR : (rank + 1) * PAIR, :]
                sums[wanted] += rows.astype(f32)

    total_rows = jnp.zeros(panel.shape, f32)
    for lane in range(LANES):
        total_rows += returned[lane, slots * PAIR :, :].astype(f32)
    panel[...] = total_rows

    def spread(number, carry):
        to = global_block[number]

        @pl.when(to >= 0)
        def _():
            for half in range(2):
                sums[to, pl.ds(global_row[number] + half * BLOCK, 1), :] += panel[
                    pl.ds(number + half * room, 1), :
                ]

        return carry

    lax.fori_loop(0, room, spread, 0)
    lane_grads[...] = sums[...].astype(lane_grads.dtype)


def finish_kernel(
    key_grad,
    value_grad,
    from_left,
    from_right,
    others,
    key_out,
    value_out,
    key_sum,
    value_sum,
):
    tokens = key_out.shape[0]
    f32 = jnp.float32

    def own(block, carry):
        row = pl.multiple_of(block * BLOCK, BLOCK)
        here, padded = pl.ds(row, BLOCK), pl.ds(row + BLOCK, BLOCK)
        key_sum[here, :] = key_grad[padded, :] + others[block, :BLOCK, :].astype(f32)
        value_sum[here, :] = value_grad[padded, :] + others[block, BLOCK:, :].astype(f32)
        return carry

    lax.fori_loop(0, others.shape[0], own, 0)
    key_sum[:BLOCK, :] += from_left[:BLOCK, :].astype(f32)
    value_sum[:BLOCK, :] += from_left[BLOCK:, :].astype(f32)
    key_sum[tokens - BLOCK :, :] += from_right[:BLOCK, :].astype(f32)
    value_sum[tokens - BLOCK :, :] += from_right[BLOCK:, :].astype(f32)

    key_out[...] = key_sum[...].astype(key_out.dtype)
    value_out[...] = value_sum[...].astype(value_out.dtype)


def exchange(array, axis):
    return lax.all_to_all(array, axis, split_axis=0, concat_axis=0, tiled=True)


def spread(array, axis):
    return exchange(jnp.broadcast_to(array, (lax.axis_size(axis),) + array.shape), axis)


def shards(queries, key_states, value_states, out_weight, output_grad, rand_blocks, global_pos):
    bf16, f32 = jnp.bfloat16, jnp.float32
    tokens, columns = queries.shape
    blocks = tokens // BLOCK
    slabs, heads = lax.axis_size("slab"), lax.axis_size("head")
    slab, me, head = lax.axis_index("slab"), lax.axis_index("lane"), lax.axis_index("head")
    position, seq_count = slab * LANES + me, slabs * LANES
    smem, vmem = whole(pltpu.SMEM), whole()

    own = jnp.concatenate(
        [key_states.reshape(blocks, BLOCK, columns), value_states.reshape(blocks, BLOCK, columns)],
        axis=1,
    )
    lane_blocks = lax.all_gather(own, "slab", axis=0, tiled=True)

    names = rand_blocks.reshape(-1)
    owner = names // blocks
    lane, code = owner % LANES, owner // LANES * blocks + names % blocks
    number = jnp.arange(names.shape[0])
    same = (lane[:, None] == lane[None, :]) & (number[None, :] < number[:, None])
    ranks = jnp.sum(same.astype(jnp.int32), axis=1)
    index = jnp.arange(LANES * slabs)
    hit = (lane * slabs + ranks)[None, :] == index[:, None]
    wanted = jnp.max(jnp.where(hit, code[None, :], -1), axis=1).reshape(LANES, slabs)
    load = jnp.broadcast_to(jnp.max(ranks) + 1, (LANES, 1))
    global_lane = global_pos // tokens % LANES
    number = jnp.arange(GLOBALS)
    same = (global_lane[:, None] == global_lane[None, :]) & (number[None, :] < number[:, None])
    global_rank = jnp.sum(same.astype(jnp.int32), axis=1)
    hit = (global_rank[None, :] == number[:, None]) & (global_lane == me)[None, :]
    global_block = global_pos // tokens // LANES * blocks + global_pos % tokens // BLOCK
    global_block = jnp.max(jnp.where(hit, global_block[None, :], -1), axis=1)
    global_row = jnp.max(jnp.where(hit, (global_pos % BLOCK)[None, :], 0), axis=1)
    heard = exchange(jnp.concatenate([wanted, load], axis=1), "lane")
    asked = heard[:, :slabs].reshape(-1)
    load = jnp.max(spread(jnp.max(heard[:, slabs:]).reshape(1), "slab"))
    choice = jnp.sum((load > jnp.array(FEW)).astype(jnp.int32))
    choice = jnp.where(jnp.max(global_rank) < FEW_ROWS, choice, len(FEW))

    partial_grad = lax.dot_general(
        output_grad, out_weight, (((1,), (1,)), ((), ())), preferred_element_type=f32
    )
    partial_grad = partial_grad.reshape(tokens, heads, columns).transpose(1, 0, 2)
    grad_att = jnp.sum(exchange(partial_grad, "head"), axis=0).astype(bf16)

    seq = ("slab", "lane")
    forth = [(i, i + 1) for i in range(seq_count - 1)]
    back = [(i + 1, i) for i in range(seq_count - 1)]
    left = lax.ppermute(own[blocks - 1], seq, forth)
    right = lax.ppermute(own[0], seq, back)

    order = (head - jnp.arange(heads)) % heads
    weight_rows = out_weight.reshape(heads, columns, -1).at[order].get(mode="promise_in_bounds")
    weight_rows = weight_rows.reshape(out_weight.shape)
    beside = (lane_blocks, asked, choice, grad_att, left, right, weight_rows)
    beside = lax.optimization_barrier(beside + (global_lane, global_rank, global_block, global_row))
    lane_blocks, asked, choice, grad_att, left, right, weight_rows = beside[:7]
    global_lane, global_rank, global_block, global_row = beside[7:]
    place = jnp.stack([position * blocks, seq_count * blocks - 1]).astype(jnp.int32)
    padded = tokens + PAIR

    def middle(slots, room):
        sent_rows = slots * PAIR + 2 * room
        global_place = (global_lane * room + global_rank).reshape(GLOBALS, 1)
        served = call(
            serve_kernel,
            shape((LANES, sent_rows, columns), bf16),
            [smem, smem, smem, vmem],
            [pltpu.VMEM((2 * room, columns), f32)],
            moved=8 << 20,
        )(asked, global_block, global_row, lane_blocks)
        arrived = exchange(served, "lane")
        attended, query_grad, key_part, value_part, rims, sent = call(
            attention_kernel,
            (
                shape((tokens, columns), bf16),
                shape((tokens, columns), bf16),
                shape((padded, columns), f32),
                shape((padded, columns), f32),
                shape((2, PAIR, columns), bf16),
                shape((LANES, sent_rows, columns), bf16),
            ),
            [smem, smem, smem] + [vmem] * 8,
            [pltpu.VMEM((padded, columns), bf16)] * 2
            + [
                pltpu.VMEM((2 * GLOBALS, columns), bf16),
                pltpu.VMEM((2 * GLOBALS, columns), f32),
            ],
            flops=1 << 30,
            moved=12 << 20,
        )(
            place,
            names,
            ranks,
            queries,
            grad_att,
            key_states,
            value_states,
            left,
            right,
            global_place,
            arrived,
        )
        returned = exchange(sent, "lane")

        pieces = [attended] + [
            lax.ppermute(attended, "head", [(i, (i + k) % heads) for i in range(heads)])
            for k in range(1, heads)
        ]
        from_left = lax.ppermute(rims[1], seq, forth)
        from_right = lax.ppermute(rims[0], seq, back)
        everywhere = jnp.concatenate(pieces, axis=1)
        weight_part = lax.dot_general(
            everywhere, output_grad, (((0,), (0,)), ((), ())), preferred_element_type=f32
        ) * (1.0 / math.sqrt(tokens * seq_count))
        returned, from_left, from_right, weight_part = lax.optimization_barrier(
            (returned, from_left, from_right, weight_part)
        )
        lane_grads = call(
            collect_kernel,
            shape((slabs * blocks, PAIR, columns), bf16),
            [smem, smem, smem, vmem],
            [
                pltpu.VMEM((slabs * blocks, PAIR, columns), f32),
                pltpu.VMEM((2 * room, columns), f32),
            ],
            moved=10 << 20,
        )(asked, global_block, global_row, returned)
        return (
            everywhere,
            query_grad,
            key_part,
            value_part,
            from_left,
            from_right,
            weight_part,
            lane_grads,
        )

    branches = [functools.partial(middle, slots, FEW_ROWS) for slots in FEW]
    branches.append(functools.partial(middle, slabs, GLOBALS))
    everywhere, query_grad, key_part, value_part, from_left, from_right, weight_part, lane_grads = (
        lax.switch(choice, branches)
    )
    others = lax.psum_scatter(lane_grads, "slab", scatter_dimension=0, tiled=True)

    weight_part = weight_part.reshape(LANES, -1, weight_part.shape[1])
    step = LANES // 2
    while step:
        pair = weight_part.reshape((2, step) + weight_part.shape[1:])
        mine = me // step % 2
        kept = lax.dynamic_index_in_dim(pair, mine, 0, keepdims=False)
        other = lax.dynamic_index_in_dim(pair, 1 - mine, 0, keepdims=False)
        other = lax.ppermute(other, "lane", [(i, i ^ step) for i in range(LANES)])
        weight_part = kept + other
        step //= 2
    features = weight_part.shape[-1]
    share = jnp.sum(exchange(weight_part.reshape(slabs, -1, features), "slab"), axis=0)
    share = spread(share, "slab").reshape(-1, features)
    weight_grad = spread(share, "lane").reshape(heads, columns, features)
    weight_grad = weight_grad.at[order].get(mode="promise_in_bounds")
    weight_grad = weight_grad.reshape(heads * columns, features)

    projected = jnp.dot(everywhere, weight_rows, preferred_element_type=f32).astype(bf16)
    key_grad, value_grad = call(
        finish_kernel,
        (shape((tokens, columns), bf16), shape((tokens, columns), bf16)),
        [vmem] * 5,
        [pltpu.VMEM((tokens, columns), f32)] * 2,
        moved=2 << 20,
    )(key_part, value_part, from_left, from_right, others)
    return projected, query_grad, key_grad, value_grad, weight_grad


def solution(mesh):
    seq_count, head_count = mesh.devices.shape
    fine = Mesh(
        mesh.devices.reshape(seq_count // LANES, LANES, head_count), ("slab", "lane", "head")
    )
    seq = ("slab", "lane")
    placed = (
        P(seq, "head"),
        P(seq, "head"),
        P(seq, "head"),
        P(None, "head"),
        P(seq, "head"),
        P(seq, None),
        P(),
    )
    return jax.shard_map(
        shards,
        mesh=fine,
        in_specs=placed,
        out_specs=(
            P(seq, "head"),
            P(seq, "head"),
            P(seq, "head"),
            P(seq, "head"),
            P(None, "head"),
        ),
        check_vma=False,
    )
```
